32 devices in a mesh: segment: 8 (over z, core), space: 2 (over x), ens: 2 (over y).
Axes of the slice: x: 2, y: 2, z: 4, core: 2. Of those that a mesh axis runs over, the one named last changes fastest.
Arguments:
- state_in: bfloat16 [2, 8, 1, 12, 180, 768], P('ens', 'segment', None, 'space'), may hold values from -6 to 6
- member_ids: int32 [2, 8, 1], P('ens'), may hold values from 0 to 99
- member_table: bfloat16 [100, 768], replicated, may hold values from -3 to 3
- pos_embed: bfloat16 [12, 180, 768], P('space'), may hold values from -3 to 3
- readout_tile_matrix: bfloat16 [768, 1280], replicated, may hold values from -0.21875 to 0.21875
- tile_lifting_matrix: bfloat16 [1280, 768], replicated, may hold values from -0.15625 to 0.15625
- norm_gain: float32 [8, 2, 768], P('segment'), may hold values from 0.5 to 1.5
- norm_shift: float32 [8, 2, 768], P('segment'), may hold values from -1.25 to 1.25
- spectral: float32 [8, 2, 2, 8, 96, 96], P('segment'), may hold values from -0.4375 to 0.4375
- up_weight: bfloat16 [8, 768, 3072], P('segment', ('space', 'ens')), may hold values from -0.21875 to 0.21875
- down_weight: bfloat16 [8, 3072, 768], P('segment', ('space', 'ens')), may hold values from -0.109375 to 0.109375
Outputs:
- state_out: bfloat16 [2, 8, 1, 12, 180, 768], P('ens', 'segment', None, 'space')
The draws below stay inside these ranges and needn't reach their ends.
All inputs are finite; a program needn't handle non-finite values.
Results may differ from the reference program's by a relative error of at most 0.0035.
Values may be sent and summed in bfloat16 or wider, within the bound.
No kernel may reach another device: no remote copies, remote signals or barrier semaphores. Data moves between devices by JAX's collectives and lax.ppermute only.
A program may use at most 128 MiB of HBM per device.

```python
import math
import jax
import jax.numpy as jnp
from jax import lax

D = 768
HID = 3072
NB = 8
C_PATCH = 1280
LON = 180
KW = 88
ENSEMBLE = 100
SECTIONS = 1
MB_SLOT = 1
BS = 96
H = 12
SEGMENTS = 8
GROUPS = 2


def plant(values, stream_key, low, top_value):
    longest = values.shape.index(max(values.shape))
    spots = []
    for shift in (0, 1):
        where = [jax.random.randint(jax.random.fold_in(stream_key, axis), (), 0, length) for axis, length in enumerate(values.shape)]
        where[longest] = (where[longest] + shift) % values.shape[longest]
        spots.append(tuple(where))
    return values.at[spots[0]].set(low).at[spots[1]].set(top_value)


def level_of(key, shape, split, smallest, high):
    level = 1.0
    for position, shards_of in split:
        heights = jax.random.uniform(jax.random.fold_in(jax.random.fold_in(key, 6), position), (shards_of,), jnp.float32, smallest / len(split), high / len(split))
        level = level * jnp.repeat(jnp.exp(heights), shape[position] // shards_of).reshape((-1,) + (1,) * (len(shape) - 1 - position))
    return level


def gaussian(key, shape, width, bound, shards=(), kind=jnp.bfloat16):
    values = jax.random.normal(key, shape, jnp.float32) * width
    if len(shards) > 0:
        values = level_of(key, shape, shards, -0.22, 0.18) * values
    return jnp.clip(values, min=-bound, max=bound).astype(kind)


def setup_inputs(seed: int = 0) -> dict:
    keys = jax.random.split(jax.random.key(seed), 12)
    return {
        "state_in": gaussian(keys[0], (GROUPS, SEGMENTS, MB_SLOT, H, LON, D), 1.0, 6.0, ((0, 2), (1, 8), (3, 2))),
        "member_ids": plant(jax.random.randint(keys[1], (GROUPS, SEGMENTS, MB_SLOT), 0, ENSEMBLE), jax.random.fold_in(keys[1], 1), 0, ENSEMBLE - 1).astype(jnp.int32),
        "member_table": gaussian(keys[2], (ENSEMBLE, D), 0.5, 3.0),
        "pos_embed": gaussian(keys[3], (H, LON, D), 0.5, 3.0, ((0, 2),)),
        "readout_tile_matrix": gaussian(keys[4], (D, C_PATCH), D ** -0.5, 0.21875),
        "tile_lifting_matrix": gaussian(keys[5], (C_PATCH, D), C_PATCH ** -0.5, 0.15625),
        "norm_gain": jnp.clip(1.0 + 0.1 * jax.random.normal(keys[6], (SEGMENTS, 2, D), jnp.float32), 0.5, 1.5),
        "norm_shift": gaussian(keys[7], (SEGMENTS, 2, D), 0.2, 1.25, ((0, 8),), jnp.float32),
        "spectral": gaussian(keys[8], (SEGMENTS, 2, 2, NB, BS, BS), (2 * BS) ** -0.5, 0.4375, ((0, 8),), jnp.float32),
        "up_weight": gaussian(keys[9], (SEGMENTS, D, HID), D ** -0.5, 0.21875, ((0, 8), (1, 4))),
        "down_weight": gaussian(keys[10], (SEGMENTS, HID, D), HID ** -0.5, 0.109375, ((0, 8), (1, 4))),
    }


EPSILON = 1e-05
SHRINK_LEVEL = 0.01
HIGHEST_PRECISION = lax.Precision.HIGHEST

def layer_norm(values):
    average = lax.optimization_barrier(jnp.mean(values, axis=-1, keepdims=True))
    centred = values - average
    spread = lax.optimization_barrier(jnp.mean(centred * centred, axis=-1, keepdims=True))
    return centred * lax.rsqrt(spread + EPSILON)

def longitude_tables(longitudes, kept, latitudes):
    number = jnp.arange(kept, dtype=jnp.int32)[:, None]
    points = jnp.arange(longitudes, dtype=jnp.int32)[None, :]
    angles = (number * points % longitudes).astype(jnp.float32) * (2.0 * math.pi / longitudes)
    factor = 1.0 / math.sqrt(latitudes * longitudes)
    doubled = jnp.where(number == 0, 1.0, 2.0).astype(jnp.float32) * factor
    forward = jnp.stack([jnp.cos(angles) * factor, -jnp.sin(angles) * factor])
    backward = jnp.stack([jnp.cos(angles) * doubled, -jnp.sin(angles) * doubled])
    return (forward, backward)

def latitude_tables(latitudes):
    number = jnp.arange(latitudes, dtype=jnp.int32)[:, None]
    points = jnp.arange(latitudes, dtype=jnp.int32)[None, :]
    angles = (number * points % latitudes).astype(jnp.float32) * (2.0 * math.pi / latitudes)
    cosine_table = jnp.cos(angles)
    sine_table = jnp.sin(angles)
    forward = jnp.concatenate([jnp.concatenate([cosine_table, sine_table], 1), jnp.concatenate([-sine_table, cosine_table], 1)], 0)
    backward = jnp.concatenate([jnp.concatenate([cosine_table, -sine_table], 1), jnp.concatenate([sine_table, cosine_table], 1)], 0)
    return (forward, backward)

def mix_blocks(spectra, filters):
    extent = spectra.shape
    halves = spectra.reshape(extent[0], 2, extent[2], extent[3], filters.shape[2], filters.shape[3])
    nonimaginary_component = halves[:, 0]
    imag_part = halves[:, 1]

    def product(operand, matrix):
        return jnp.einsum('mhknb,nbc->mhknc', operand, matrix, precision=HIGHEST_PRECISION)
    first_real = jax.nn.relu(product(nonimaginary_component, filters[0, 0]) - product(imag_part, filters[0, 1]))
    first_imag = jax.nn.relu(product(nonimaginary_component, filters[0, 1]) + product(imag_part, filters[0, 0]))
    second_real = product(first_real, filters[1, 0]) - product(first_imag, filters[1, 1])
    second_imag = product(first_real, filters[1, 1]) + product(first_imag, filters[1, 0])
    blended = jnp.stack([second_real, second_imag], axis=1)
    blended = blended - jnp.clip(blended, -SHRINK_LEVEL, SHRINK_LEVEL)
    return blended.reshape(extent)

def block_update(carried, gains, shifts, filters, up_matrix, down_matrix, tables):
    forward, backward, lat_forward, lat_backward = tables
    channels = carried.shape[-1]
    normed_one = layer_norm(carried) * gains[0] + shifts[0]
    spectra = jnp.einsum('rkw,mhwd->mrhkd', forward, normed_one, precision=HIGHEST_PRECISION)
    extent = spectra.shape
    stacked = spectra.reshape(extent[0], 2 * extent[2], extent[3], extent[4])
    turned = jnp.einsum('ab,mbkd->makd', lat_forward, stacked, precision=HIGHEST_PRECISION)
    blended_modes = mix_blocks(turned.reshape(extent), filters).reshape(stacked.shape)
    inverse = jnp.einsum('ab,mbkd->makd', lat_backward, blended_modes, precision=HIGHEST_PRECISION).reshape(extent)
    filtered = jnp.einsum('rkw,mrhkd->mhwd', backward, inverse, precision=HIGHEST_PRECISION)
    blended = carried + normed_one + filtered
    normed_two = (layer_norm(blended) * gains[1] + shifts[1]).astype(jnp.bfloat16)
    flat_rows = normed_two.reshape(-1, channels)
    hidden = jax.nn.gelu(jnp.dot(flat_rows, up_matrix, preferred_element_type=jnp.float32), approximate=False).astype(jnp.bfloat16)
    update = jnp.dot(hidden, down_matrix, preferred_element_type=jnp.float32).reshape(blended.shape)
    return (blended + update).astype(jnp.bfloat16)

def reference(state_in, member_ids, member_table, pos_embed, readout_tile_matrix, tile_lifting_matrix, norm_gain, norm_shift, spectral, up_weight, down_weight):
    forward, backward = longitude_tables(LON, KW, H)
    lat_forward, lat_backward = latitude_tables(H)
    tables = (forward, backward, lat_forward, lat_backward)
    states = state_in
    groups = states.shape[0]
    segments = states.shape[1]
    micro_count = states.shape[2]
    for section in range(SECTIONS):
        ids_now = jnp.roll(member_ids, section, axis=1)

        def one_segment(inputs):
            location, incoming, chosen, gains, shifts, filters, up_matrix, down_matrix = inputs
            merged = incoming.reshape((groups * micro_count,) + incoming.shape[2:])
            sample_trajectory_lines = member_table[chosen.reshape(-1)].astype(jnp.float32)

            def enter_grid(values):
                standardized_field = layer_norm(values.astype(jnp.float32)).astype(jnp.bfloat16)
                prediction_increment = jnp.einsum('fbrd,do->fbro', standardized_field, readout_tile_matrix, preferred_element_type=jnp.float32).astype(jnp.bfloat16)
                admitted_lines = jnp.einsum('nzwt,tl->nzwl', prediction_increment, tile_lifting_matrix, preferred_element_type=jnp.float32)
                return admitted_lines + pos_embed.astype(jnp.float32)[None] + sample_trajectory_lines[:, None, None, :]

            def cast_values(values):
                return values.astype(jnp.float32)
            carried = lax.cond(location == 0, enter_grid, cast_values, merged)
            result = block_update(carried, gains, shifts, filters, up_matrix, down_matrix, tables)
            return result.reshape(incoming.shape)
        advanced = lax.map(one_segment, (jnp.arange(segments, dtype=jnp.int32), jnp.moveaxis(states, 1, 0), jnp.moveaxis(ids_now, 1, 0), norm_gain, norm_shift, spectral, up_weight, down_weight))
        states = jnp.roll(jnp.moveaxis(advanced, 0, 1), 1, axis=1)
    return states
```

```python
import functools
import math

import jax
import jax.numpy as jnp
import ml_dtypes
import numpy as np
from jax import lax
from jax.experimental import pallas as pl
from jax.experimental.pallas import tpu as pltpu
from jax.sharding import PartitionSpec as P

KW = 88


EPSILON = 1e-05
SHRINK_LEVEL = 0.01
HIGHEST_PRECISION = lax.Precision.HIGHEST


def shifted(value, axis, steps):
    count = lax.axis_size(axis)
    pairs = [(source, (source + steps) % count) for source in range(count)]
    return lax.ppermute(value, axis, pairs)


def layer_norm(values):
    average = jnp.mean(values, axis=-1, keepdims=True)
    centred = values - average
    spread = jnp.mean(centred * centred, axis=-1, keepdims=True)
    return centred * lax.rsqrt(spread + EPSILON)


def longitude_tables(longitudes, kept, latitudes):
    number = jnp.arange(kept, dtype=jnp.int32)[:, None]
    points = jnp.arange(longitudes, dtype=jnp.int32)[None, :]
    angles = (number * points % longitudes).astype(jnp.float32) * (2.0 * math.pi / longitudes)
    factor = 1.0 / math.sqrt(latitudes * longitudes)
    doubled = jnp.where(number == 0, 1.0, 2.0).astype(jnp.float32) * factor
    forward = jnp.stack([jnp.cos(angles) * factor, -jnp.sin(angles) * factor])
    backward = jnp.stack([jnp.cos(angles) * doubled, -jnp.sin(angles) * doubled])
    return (forward, backward)


def latitude_tables(latitudes):
    number = jnp.arange(latitudes, dtype=jnp.int32)[:, None]
    points = jnp.arange(latitudes, dtype=jnp.int32)[None, :]
    angles = (number * points % latitudes).astype(jnp.float32) * (2.0 * math.pi / latitudes)
    cosine_table = jnp.cos(angles)
    sine_table = jnp.sin(angles)
    forward = jnp.concatenate(
        [
            jnp.concatenate([cosine_table, sine_table], 1),
            jnp.concatenate([-sine_table, cosine_table], 1),
        ],
        0,
    )
    backward = jnp.concatenate(
        [
            jnp.concatenate([cosine_table, -sine_table], 1),
            jnp.concatenate([sine_table, cosine_table], 1),
        ],
        0,
    )
    return (forward, backward)


def mix_blocks(spectra, filters):
    extent = spectra.shape
    halves = spectra.reshape(extent[0], 2, extent[2], extent[3], filters.shape[2], filters.shape[3])
    nonimaginary_component = halves[:, 0]
    imag_part = halves[:, 1]

    def product(operand, matrix):
        return jnp.einsum("mhknb,nbc->mhknc", operand, matrix, precision=HIGHEST_PRECISION)

    first_real = jax.nn.relu(
        product(nonimaginary_component, filters[0, 0]) - product(imag_part, filters[0, 1])
    )
    first_imag = jax.nn.relu(
        product(nonimaginary_component, filters[0, 1]) + product(imag_part, filters[0, 0])
    )
    second_real = product(first_real, filters[1, 0]) - product(first_imag, filters[1, 1])
    second_imag = product(first_real, filters[1, 1]) + product(first_imag, filters[1, 0])
    blended = jnp.stack([second_real, second_imag], axis=1)
    blended = blended - jnp.clip(blended, -SHRINK_LEVEL, SHRINK_LEVEL)
    return blended.reshape(extent)


def spectral_filter(normed_one, filters, tables):
    forward, backward, lat_forward, lat_backward = tables
    spectra = jnp.einsum("rkw,mhwd->mrhkd", forward, normed_one, precision=HIGHEST_PRECISION)
    collected_fields = lax.all_to_all(spectra, "space", split_axis=3, concat_axis=2, tiled=True)
    extent = collected_fields.shape
    stacked = collected_fields.reshape(extent[0], 2 * extent[2], extent[3], extent[4])
    turned = jnp.einsum("ab,mbkd->makd", lat_forward, stacked, precision=HIGHEST_PRECISION)
    blended_modes = mix_blocks(turned.reshape(extent), filters).reshape(stacked.shape)
    inverse = jnp.einsum(
        "ab,mbkd->makd", lat_backward, blended_modes, precision=HIGHEST_PRECISION
    ).reshape(extent)
    returned = lax.all_to_all(inverse, "space", split_axis=2, concat_axis=3, tiled=True)
    return jnp.einsum("rkw,mrhkd->mhwd", backward, returned, precision=HIGHEST_PRECISION)


def on_device(
    state_in,
    member_ids,
    member_table,
    pos_embed,
    readout_tile_matrix,
    tile_lifting_matrix,
    norm_gain,
    norm_shift,
    spectral,
    up_weight,
    down_weight,
):
    position = lax.axis_index("segment")
    segment_count = lax.axis_size("segment")
    current = state_in[0, 0]
    channels = current.shape[3]
    latitudes = current.shape[1] * lax.axis_size("space")
    forward, backward = longitude_tables(current.shape[2], KW, latitudes)
    lat_forward, lat_backward = latitude_tables(latitudes)
    tables = (forward, backward, lat_forward, lat_backward)
    gains = norm_gain[0]
    shifts = norm_shift[0]
    filters = spectral[0]
    slot_index = -0 % segment_count
    chosen = member_ids[0, slot_index]
    onehot = (
        chosen[:, None] == jnp.arange(member_table.shape[0], dtype=jnp.int32)[None, :]
    ).astype(jnp.bfloat16)
    sample_trajectory_lines = jnp.dot(onehot, member_table, preferred_element_type=jnp.float32)

    def enter_grid(values):
        standardized_field = layer_norm(values.astype(jnp.float32)).astype(jnp.bfloat16)
        prediction_increment = jnp.einsum(
            "fbrd,do->fbro",
            standardized_field,
            readout_tile_matrix,
            preferred_element_type=jnp.float32,
        ).astype(jnp.bfloat16)
        admitted_lines = jnp.einsum(
            "nzwt,tl->nzwl",
            prediction_increment,
            tile_lifting_matrix,
            preferred_element_type=jnp.float32,
        )
        return (
            admitted_lines
            + pos_embed.astype(jnp.float32)[None]
            + sample_trajectory_lines[:, None, None, :]
        )

    def cast_values(values):
        return values.astype(jnp.float32)

    carried = lax.cond(position == 0, enter_grid, cast_values, current)
    normed_one = layer_norm(carried) * gains[0] + shifts[0]
    blended = carried + normed_one + spectral_filter(normed_one, filters, tables)
    normed_two = (layer_norm(blended) * gains[1] + shifts[1]).astype(jnp.bfloat16)
    flat_rows = normed_two.reshape(-1, channels)
    columns = flat_rows
    lifted = jnp.dot(
        columns,
        lax.all_gather(up_weight, ("space", "ens"), axis=1, tiled=True)[0],
        preferred_element_type=jnp.float32,
    )
    hidden = jax.nn.gelu(lifted, approximate=False).astype(jnp.bfloat16)
    columns = hidden
    update = jnp.dot(
        columns,
        lax.all_gather(down_weight, ("space", "ens"), axis=1, tiled=True)[0],
        preferred_element_type=jnp.float32,
    ).reshape(blended.shape)
    current = shifted((blended + update).astype(jnp.bfloat16), "segment", 1)
    return current[None, None]


ROW_STEP = 192
GROUP_LANES = 128
MESH_AXES = ("segment", "space", "ens")


def split_table(table):
    high = table.astype(ml_dtypes.bfloat16)
    low = (table - high.astype(np.float64)).astype(ml_dtypes.bfloat16)
    return np.stack([high, low])


def split_longitude_tables(longitudes, kept, latitudes):
    number = np.arange(kept)[:, None]
    points = np.arange(longitudes)[None, :]
    angles = (number * points % longitudes) * (2.0 * math.pi / longitudes)
    factor = 1.0 / math.sqrt(latitudes * longitudes)
    doubled = np.where(number == 0, 1.0, 2.0) * factor
    forward = np.concatenate([np.cos(angles) * factor, -np.sin(angles) * factor], 0)
    backward = np.concatenate([np.cos(angles) * doubled, -np.sin(angles) * doubled], 0).T
    return split_table(forward), split_table(backward)


def three_point(x, sign):
    (ar, ai), (br, bi), (cr, ci) = x
    tr, ti = br + cr, bi + ci
    mr, mi = ar - 0.5 * tr, ai - 0.5 * ti
    scale = math.sin(math.pi / 3.0) * sign
    dr, di = (br - cr) * scale, (bi - ci) * scale
    return [(ar + tr, ai + ti), (mr - di, mi + dr), (mr + di, mi - dr)]


def four_point(x, sign):
    (ar, ai), (br, bi), (cr, ci), (dr, di) = x
    sr, si, tr, ti = ar + cr, ai + ci, ar - cr, ai - ci
    ur, ui, vr, vi = br + dr, bi + di, br - dr, bi - di
    plus, minus = (tr - vi, ti + vr), (tr + vi, ti - vr)
    if sign < 0:
        plus, minus = minus, plus
    return [(sr + ur, si + ui), plus, (sr - ur, si - ui), minus]


def twelve_point(x, sign):
    columns = [three_point([x[(4 * a + 3 * b) % 12] for a in range(3)], sign) for b in range(4)]
    out = [None] * 12
    for a in range(3):
        line = four_point([columns[b][a] for b in range(4)], sign)
        for b in range(4):
            out[(4 * a + 9 * b) % 12] = line[b]
    return out


def lane_index(shape):
    return lax.broadcasted_iota(jnp.int32, shape, len(shape) - 1)


def spread_groups(values):
    a, b, c = (values[:, 128 * i : 128 * i + 128] for i in range(3))
    lanes = lane_index(a.shape)
    second = jnp.where(lanes < 32, pltpu.roll(a, 32, 1), pltpu.roll(b, 32, 1))
    third = jnp.where(lanes < 64, pltpu.roll(b, 64, 1), pltpu.roll(c, 64, 1))
    return jnp.concatenate([a, second, third, pltpu.roll(c, 96, 1)], 1)


def gather_groups(values):
    a, b, c, d = (values[:, 128 * i : 128 * i + 128] for i in range(4))
    lanes = lane_index(a.shape)
    first = jnp.where(lanes < 96, a, pltpu.roll(b, 96, 1))
    second = jnp.where(lanes < 64, pltpu.roll(b, 96, 1), pltpu.roll(c, 64, 1))
    third = jnp.where(lanes < 32, pltpu.roll(c, 64, 1), pltpu.roll(d, 32, 1))
    return jnp.concatenate([first, second, third], 1)


def gelu(x):
    return 0.5 * x * (1.0 + lax.erf(x * math.sqrt(0.5)))


def enter_kernel(
    scalars_ref,
    state_ref,
    readout_hbm,
    lifting_hbm,
    pos_hbm,
    table_hbm,
    out_ref,
    readout_ref,
    lifting_ref,
    pos_ref,
    table_ref,
    rows_ref,
    sems,
):
    first_segment, member = scalars_ref[0] == 0, scalars_ref[1]
    rows, width = state_ref.shape[:2]

    @pl.when(first_segment)
    def _():
        pairs = (
            (readout_hbm, readout_ref),
            (lifting_hbm, lifting_ref),
            (pos_hbm, pos_ref),
            (table_hbm, table_ref),
        )
        loads = [
            pltpu.make_async_copy(source, target, sems.at[number])
            for number, (source, target) in enumerate(pairs)
        ]
        for load in loads:
            load.start()
        rows_ref[...] = jnp.zeros_like(rows_ref)
        for row in range(rows):
            normed = layer_norm(state_ref[row].astype(jnp.float32)).astype(jnp.bfloat16)
            rows_ref[pl.ds(ROW_STEP * row, width)] = normed
        loads[0].wait()
        loads[3].wait()
        members = table_ref.shape[0]
        chosen = lax.broadcasted_iota(jnp.int32, (8, members), 1) == member
        line = jnp.dot(
            jnp.where(chosen, 1.0, 0.0).astype(jnp.bfloat16),
            table_ref[...],
            preferred_element_type=jnp.float32,
        )[0:1]
        for first in range(0, rows, 2):
            block = rows_ref[pl.ds(ROW_STEP * first, 2 * ROW_STEP)]
            forecast = jnp.dot(block, readout_ref[...], preferred_element_type=jnp.float32)
            if first == 0:
                loads[1].wait()
                loads[2].wait()
            lifted = jnp.dot(
                forecast.astype(jnp.bfloat16), lifting_ref[...], preferred_element_type=jnp.float32
            )
            for row in range(2):
                part = lifted[ROW_STEP * row : ROW_STEP * row + width]
                carried = part + pos_ref[first + row].astype(jnp.float32) + line
                out_ref[first + row] = carried.astype(jnp.bfloat16)

    @pl.when(jnp.logical_not(first_segment))
    def _():
        out_ref[...] = state_ref[...]


def filter_kernel(
    scalars_ref,
    own_ref,
    other_ref,
    norms_ref,
    forward_ref,
    backward_ref,
    first_ref,
    second_ref,
    out_ref,
    grid_ref,
    modes_ref,
):
    half = scalars_ref[0]
    lower = half == 0
    rows = own_ref.shape[0]
    channels = own_ref.shape[2] // 2
    kept = grid_ref.shape[1] // 2
    groups = modes_ref.shape[0]
    bases = (half * rows, (1 - half) * rows)

    def dot(a, b):
        return jnp.dot(a, b, preferred_element_type=jnp.float32)

    def chosen(values):
        return jnp.where(lower, values[:, :channels], values[:, channels:])

    gain, shift = chosen(norms_ref[0:1]), chosen(norms_ref[2:3])
    for row in range(rows):
        for source, base in zip((own_ref, other_ref), bases):
            values = source[row].astype(jnp.float32)
            average = jnp.mean(values, axis=-1, keepdims=True)
            centred = values - average
            spread = jnp.mean(centred * centred, axis=-1, keepdims=True)
            normed = chosen(centred) * lax.rsqrt(spread + EPSILON) * gain + shift
            points = spread_groups(normed).astype(jnp.bfloat16)
            grid_ref[base + row] = dot(forward_ref[0], points) + dot(forward_ref[1], points)

    def turn(step, carry):
        low = pl.multiple_of(step * 8, 8)
        for group in range(groups):
            lanes = pl.ds(GROUP_LANES * group, GROUP_LANES)
            values = [
                (grid_ref[h, pl.ds(low, 8), lanes], grid_ref[h, pl.ds(kept + low, 8), lanes])
                for h in range(12)
            ]
            for k, (real, imag) in enumerate(twelve_point(values, -1)):
                at = pl.ds(k * kept + low, 8)
                modes_ref[group, at, pl.ds(0, GROUP_LANES)] = real
                modes_ref[group, at, pl.ds(GROUP_LANES, GROUP_LANES)] = imag
        return carry

    lax.fori_loop(0, kept // 8, turn, 0)
    for group in range(groups):
        u = jax.nn.relu(dot(modes_ref[group].astype(jnp.bfloat16), first_ref[group]))
        v = dot(u.astype(jnp.bfloat16), second_ref[group])
        modes_ref[group] = v - jnp.clip(v, -SHRINK_LEVEL, SHRINK_LEVEL)

    def turn_back(step, carry):
        low = pl.multiple_of(step * 8, 8)
        for group in range(groups):
            lanes = pl.ds(GROUP_LANES * group, GROUP_LANES)
            values = []
            for k in range(12):
                at = pl.ds(k * kept + low, 8)
                values.append(
                    (
                        modes_ref[group, at, pl.ds(0, GROUP_LANES)],
                        modes_ref[group, at, pl.ds(GROUP_LANES, GROUP_LANES)],
                    )
                )
            for h, (real, imag) in enumerate(twelve_point(values, 1)):
                grid_ref[h, pl.ds(low, 8), lanes] = real
                grid_ref[h, pl.ds(kept + low, 8), lanes] = imag
        return carry

    lax.fori_loop(0, kept // 8, turn_back, 0)
    for part, base in enumerate(bases):
        for row in range(rows):
            spectra = grid_ref[base + row].astype(jnp.bfloat16)
            filtered = dot(backward_ref[0], spectra) + dot(backward_ref[1], spectra)
            out_ref[part * rows + row] = gather_groups(filtered).astype(out_ref.dtype)


def start_loads(near, near_refs, far_refs, targets, sems):
    def copies(refs):
        return [
            pltpu.make_async_copy(ref, target, sems.at[number])
            for number, (ref, target) in enumerate(zip(refs, targets))
        ]

    @pl.when(near)
    def _():
        for copy in copies(near_refs):
            copy.start()

    @pl.when(jnp.logical_not(near))
    def _():
        for copy in copies(far_refs):
            copy.start()

    return copies(near_refs)


def hidden_kernel(
    scalars_ref,
    own_ref,
    other_ref,
    mine_ref,
    theirs_ref,
    norms_ref,
    held_ref,
    first_ref,
    second_ref,
    third_ref,
    relayed_ref,
    blended_ref,
    hidden_ref,
    rows_ref,
    up_ref,
    sems,
):
    half, space, member = scalars_ref[0], scalars_ref[1], scalars_ref[2]
    rows, width, channels = own_ref.shape
    depth = held_ref.shape[0]
    here, away = 2 * space, 2 * (1 - space)
    order = [here + member, here + 1 - member, away + member, away + 1 - member]
    loads = start_loads(
        half == space,
        [held_ref, first_ref, second_ref, relayed_ref],
        [second_ref, third_ref, first_ref, relayed_ref],
        [up_ref.at[pl.ds(pl.multiple_of(shard * depth, depth), depth)] for shard in order],
        sems,
    )
    rows_ref[...] = jnp.zeros_like(rows_ref)

    def enter_rows(part, row):
        source = (own_ref, other_ref)[part]
        carried = source[row].astype(jnp.float32)
        normed = layer_norm(carried) * norms_ref[0:1] + norms_ref[2:3]
        mine = mine_ref[part * rows + row].astype(jnp.float32)
        theirs = theirs_ref[(1 - part) * rows + row].astype(jnp.float32)
        low = jnp.where(half == 0, mine, theirs)
        high = jnp.where(half == 0, theirs, mine)
        blended = carried + normed + jnp.concatenate([low, high], 1)
        if part == 0:
            blended_ref[row] = blended
        again = layer_norm(blended) * norms_ref[1:2] + norms_ref[3:4]
        place = row // 2 * 4 + part * 2 + row % 2
        rows_ref[pl.ds(ROW_STEP * place, width)] = again.astype(jnp.bfloat16)

    step = up_ref.shape[1] // 2
    for block in range(rows // 2):
        for part in range(2):
            for row in range(2):
                enter_rows(part, 2 * block + row)
        if block == 0:
            for copy in loads:
                copy.wait()
        at = pl.ds(4 * ROW_STEP * block, 4 * ROW_STEP)
        values = rows_ref[at]
        for column in range(0, up_ref.shape[1], step):
            lifted = jnp.dot(
                values, up_ref[:, pl.ds(column, step)], preferred_element_type=jnp.float32
            )
            hidden_ref[at, pl.ds(column, step)] = gelu(lifted).astype(jnp.bfloat16)


def update_kernel(
    number,
    scalars_ref,
    blended_ref,
    hidden_ref,
    held_ref,
    near_ref,
    far_ref,
    relayed_ref,
    own_ref,
    other_ref,
    down_ref,
    sems,
):
    half, space, member = scalars_ref[0], scalars_ref[1], scalars_ref[2]
    count, width, channels = own_ref.shape
    depth = held_ref.shape[0]
    loads = start_loads(
        half == space,
        [held_ref, near_ref],
        [far_ref, relayed_ref],
        [
            down_ref.at[pl.ds(pl.multiple_of(shard * depth, depth), depth)]
            for shard in (member, 1 - member)
        ],
        sems,
    )
    for copy in loads:
        copy.wait()
    block = hidden_ref[pl.ds(4 * ROW_STEP * number, 4 * ROW_STEP)]
    update = jnp.dot(block, down_ref[...], preferred_element_type=jnp.float32)
    for row in range(count):
        part = update[ROW_STEP * row : ROW_STEP * row + width]
        own_ref[row] = blended_ref[count * number + row] + part
        part = update[ROW_STEP * (count + row) : ROW_STEP * (count + row) + width]
        other_ref[row] = part.astype(other_ref.dtype)


def collect_kernel(relayed_ref, *refs):
    sources, out_ref, sems = refs[:-2], refs[-2], refs[-1]
    parts = (len(sources) + 1) // 2
    count = sources[0].shape[0]

    def copies(step):
        return [
            pltpu.make_async_copy(
                sources[min(2 * part + step, len(sources) - 1)],
                out_ref.at[pl.ds(count * part, count)],
                sems.at[part],
            )
            for part in range(parts)
        ]

    for step in range(2):

        @pl.when(relayed_ref[0] == step)
        def _():
            for copy in copies(step):
                copy.start()

    for copy in copies(0):
        copy.wait()


VMEM = pltpu.VMEM
SCALARS = pl.BlockSpec(memory_space=pltpu.SMEM)
WHOLE = pl.BlockSpec(memory_space=pltpu.VMEM)
LEFT = pl.BlockSpec(memory_space=pltpu.HBM)


def cost(microseconds):
    return pl.CostEstimate(
        flops=int(microseconds * 1.1e9), bytes_accessed=0, transcendentals=0
    )


def params(megabytes):
    return pltpu.CompilerParams(vmem_limit_bytes=megabytes * 2**20)


def mixing_matrix(parts):
    room = GROUP_LANES - parts.shape[-1]
    real, imag = jnp.pad(parts, ((0, 0), (0, 0), (0, room), (0, room)))
    top = jnp.concatenate([real, imag], 2)
    low = jnp.concatenate([-imag, real], 2)
    return jnp.concatenate([top, low], 1).astype(jnp.bfloat16)


def fast_on_device(
    sizes,
    state_in,
    member_ids,
    member_table,
    pos_embed,
    readout_tile_matrix,
    tile_lifting_matrix,
    norm_gain,
    norm_shift,
    spectral,
    up_weight,
    down_weight,
):
    segments, spaces, members = sizes
    position = lax.axis_index("segment")
    core = position % 2
    space = lax.axis_index("space")
    member = lax.axis_index("ens")
    near = core == space

    def table(target):
        pairs = []
        for g in range(segments):
            for s in range(spaces):
                for e in range(members):
                    to = target(g, s, e)
                    if to is not None:
                        flat = (to[0] * spaces + to[1]) * members + to[2]
                        pairs.append(((g * spaces + s) * members + e, flat))
        return pairs

    def send(value, pairs):
        return lax.ppermute(value, MESH_AXES, pairs)

    def keeps(g, s):
        return g % 2 == s

    def moved_place(g, s, e):
        return (g // 2 * 2 + s, g % 2, e)

    relocate = table(moved_place)
    far_relocate = table(lambda g, s, e: None if keeps(g, s) else moved_place(g, s, e))
    first_way = table(lambda g, s, e: (g, s, 1 - e) if keeps(g, s) else moved_place(g, s, e))
    second_way = table(lambda g, s, e: (g ^ 1, s, e) if keeps(g, s) else (g, 1 - s, e))
    third_way = table(lambda g, s, e: (g ^ 1, s, 1 - e) if keeps(g, s) else None)
    across = table(lambda g, s, e: (g, s, 1 - e))
    near_across = table(lambda g, s, e: (g, s, 1 - e) if keeps(g, s) else None)
    far_across = table(lambda g, s, e: (g, s, 1 - e) if not keeps(g, s) else None)
    swap_cores = table(lambda g, s, e: (g ^ 1, s, e))
    near_to_other = table(lambda g, s, e: (g ^ 1, s, e) if keeps(g, s) else None)
    onward = table(lambda g, s, e: ((g // 2 * 2 + s + 1) % segments, g % 2, e))
    onward_by_space = table(
        lambda g, s, e: (g, 0, e)
        if s == 1 and g % 2 == 0
        else ((g // 2 * 2 + s + 1) % segments, g % 2, e)
    )
    onward_rest = table(
        lambda g, s, e: ((g + 2) % segments, 0, e) if s == 0 and g % 2 == 0 else None
    )

    state = state_in[0, 0, 0]
    rows, width, channels = state.shape
    latitudes = rows * spaces
    bf16, f32, i32 = jnp.bfloat16, jnp.float32, jnp.int32
    up, down = up_weight[0], down_weight[0]
    hidden_half = up.shape[1] // 2
    scalars = jnp.stack([core, space, member]).astype(i32)

    up_held = lax.dynamic_slice_in_dim(up, space * hidden_half, hidden_half, 1)
    up_given = lax.dynamic_slice_in_dim(up, (1 - space) * hidden_half, hidden_half, 1)
    up_first = send(up_held, first_way)
    entered = pl.pallas_call(
        enter_kernel,
        out_shape=jax.ShapeDtypeStruct(state.shape, bf16),
        in_specs=[SCALARS, WHOLE] + [LEFT] * 4,
        out_specs=WHOLE,
        scratch_shapes=[
            VMEM(readout_tile_matrix.shape, bf16),
            VMEM(tile_lifting_matrix.shape, bf16),
            VMEM(pos_embed.shape, bf16),
            VMEM(member_table.shape, bf16),
            VMEM((rows * ROW_STEP, channels), bf16),
            pltpu.SemaphoreType.DMA((4,)),
        ],
        cost_estimate=cost(9),
        compiler_params=params(60),
    )(
        jnp.stack([position, member_ids[0, 0, 0]]).astype(i32),
        state,
        readout_tile_matrix,
        tile_lifting_matrix,
        pos_embed,
        member_table,
    )
    entered, up_first = lax.optimization_barrier((entered, up_first))
    moved = send(entered, relocate)
    down_near = send(down, near_across)
    up_third = send(up_given, third_way)

    half_groups = spectral.shape[3] // 2
    side = spectral.shape[-1]
    norms = jnp.concatenate([norm_gain[0], norm_shift[0]], 0)
    norm_lines = norms.reshape(-1, side)
    wanted = lax.dynamic_slice_in_dim(spectral[0], core * half_groups, half_groups, 2)
    offered = lax.dynamic_slice_in_dim(spectral[0], (1 - core) * half_groups, half_groups, 2)
    offered = jnp.concatenate([offered.reshape(-1, side), norm_lines], 0)
    taken = send(offered, near_to_other)
    norms = jnp.where(near, norms, taken[-norm_lines.shape[0] :].reshape(norms.shape))
    filters = jnp.where(near, wanted, taken[: -norm_lines.shape[0]].reshape(wanted.shape))
    first_matrix = mixing_matrix(filters[0])
    second_matrix = mixing_matrix(filters[1])

    moved, up_given_later, down_near, up_third = lax.optimization_barrier(
        (moved, up_given, down_near, up_third)
    )
    up_second = send(up_given_later, second_way)
    moved_other = send(moved, swap_cores)
    moved_other, up_second, norms, first_matrix, second_matrix = lax.optimization_barrier(
        (moved_other, up_second, norms, first_matrix, second_matrix)
    )
    up_relayed = send(jnp.where(near, up_second, up_first), across)
    _, down_later = lax.optimization_barrier((up_second, down))
    down_far = send(down_later, far_relocate)

    forward, backward = split_longitude_tables(width, KW, latitudes)
    lanes = half_groups * GROUP_LANES
    filtered = pl.pallas_call(
        filter_kernel,
        out_shape=jax.ShapeDtypeStruct((2 * rows, width, channels // 2), bf16),
        in_specs=[SCALARS] + [WHOLE] * 7,
        out_specs=WHOLE,
        scratch_shapes=[
            VMEM((latitudes, 2 * KW, lanes), f32),
            VMEM((half_groups, latitudes * KW, 2 * GROUP_LANES), f32),
        ],
        cost_estimate=cost(11),
        compiler_params=params(40),
    )(
        scalars,
        moved,
        moved_other,
        norms,
        jnp.asarray(forward),
        jnp.asarray(backward),
        first_matrix,
        second_matrix,
    )
    filtered, down_far, up_relayed = lax.optimization_barrier((filtered, down_far, up_relayed))
    down_relayed = send(down_far, far_across)
    filtered_other = send(filtered, swap_cores)

    parts = rows // 2
    blended, hidden = pl.pallas_call(
        hidden_kernel,
        out_shape=[
            VMEM(state.shape, f32),
            VMEM((2 * rows * ROW_STEP, hidden_half), bf16),
        ],
        in_specs=[SCALARS] + [WHOLE] * 5 + [LEFT] * 5,
        out_specs=[WHOLE] * 2,
        scratch_shapes=[
            VMEM((2 * rows * ROW_STEP, channels), bf16),
            VMEM((channels, hidden_half), bf16),
            pltpu.SemaphoreType.DMA((4,)),
        ],
        cost_estimate=cost(11),
        compiler_params=params(40),
    )(
        scalars,
        moved,
        moved_other,
        filtered,
        filtered_other,
        norms,
        up_held,
        up_first,
        up_second,
        up_third,
        up_relayed,
    )
    landed, ready = [], []
    for number in range(parts):
        if number > 1:
            scalars, _ = lax.optimization_barrier((scalars, ready[number - 2]))
        own, other = pl.pallas_call(
            functools.partial(update_kernel, number),
            out_shape=[
                jax.ShapeDtypeStruct((2, width, channels), f32),
                jax.ShapeDtypeStruct((2, width, channels), bf16),
            ],
            in_specs=[SCALARS] + [WHOLE] * 2 + [LEFT] * 4,
            out_specs=[WHOLE] * 2,
            scratch_shapes=[
                VMEM((2 * hidden_half // 2, channels), bf16),
                pltpu.SemaphoreType.DMA((2,)),
            ],
            cost_estimate=cost(4),
            compiler_params=params(24),
        )(scalars, blended, hidden, down, down_near, down_far, down_relayed)
        ready.append((own + send(other, swap_cores).astype(f32)).astype(bf16))
        if number + 1 < parts:
            first_hop = send(ready[-1], onward_by_space)
            landed.append((first_hop, send(first_hop, onward_rest)))
        else:
            landed.append((send(ready[-1], onward),))
    relayed = (core + space == 0).astype(i32)[None]
    arrived = [value for chunk in landed for value in chunk]
    out = pl.pallas_call(
        collect_kernel,
        out_shape=jax.ShapeDtypeStruct(state.shape, bf16),
        in_specs=[SCALARS] + [LEFT] * len(arrived),
        out_specs=LEFT,
        scratch_shapes=[pltpu.SemaphoreType.DMA((parts,))],
        compiler_params=params(16),
    )(relayed, *arrived)
    return out[None, None, None]


def solution(mesh):
    placed = (
        P("ens", "segment", None, "space", None, None),
        P("ens", None, None),
        P(),
        P("space", None, None),
        P(),
        P(),
        P("segment", None, None),
        P("segment", None, None),
        P("segment", None, None, None, None, None),
        P("segment", ("space", "ens"), None),
        P("segment", ("space", "ens"), None),
    )
    sizes = tuple(mesh.shape[axis] for axis in MESH_AXES)
    whole_micro_batch_on_a_chip = sizes[0] % 2 == 0 and sizes[1:] == (2, 2)
    if whole_micro_batch_on_a_chip:
        program = functools.partial(fast_on_device, sizes)
    else:
        program = on_device
    return jax.shard_map(
        program,
        mesh=mesh,
        in_specs=placed,
        out_specs=P("ens", "segment", None, "space", None, None),
        check_vma=False,
    )
```

```python
import functools
import math

import jax
import jax.numpy as jnp
import ml_dtypes
import numpy as np
from jax import lax
from jax.experimental import pallas as pl
from jax.experimental.pallas import tpu as pltpu
from jax.sharding import PartitionSpec as P

KW = 88


EPSILON = 1e-05
SHRINK_LEVEL = 0.01
HIGHEST_PRECISION = lax.Precision.HIGHEST


def shifted(value, axis, steps):
    count = lax.axis_size(axis)
    pairs = [(source, (source + steps) % count) for source in range(count)]
    return lax.ppermute(value, axis, pairs)


def layer_norm(values):
    average = jnp.mean(values, axis=-1, keepdims=True)
    centred = values - average
    spread = jnp.mean(centred * centred, axis=-1, keepdims=True)
    return centred * lax.rsqrt(spread + EPSILON)


def longitude_tables(longitudes, kept, latitudes):
    number = jnp.arange(kept, dtype=jnp.int32)[:, None]
    points = jnp.arange(longitudes, dtype=jnp.int32)[None, :]
    angles = (number * points % longitudes).astype(jnp.float32) * (2.0 * math.pi / longitudes)
    factor = 1.0 / math.sqrt(latitudes * longitudes)
    doubled = jnp.where(number == 0, 1.0, 2.0).astype(jnp.float32) * factor
    forward = jnp.stack([jnp.cos(angles) * factor, -jnp.sin(angles) * factor])
    backward = jnp.stack([jnp.cos(angles) * doubled, -jnp.sin(angles) * doubled])
    return (forward, backward)


def latitude_tables(latitudes):
    number = jnp.arange(latitudes, dtype=jnp.int32)[:, None]
    points = jnp.arange(latitudes, dtype=jnp.int32)[None, :]
    angles = (number * points % latitudes).astype(jnp.float32) * (2.0 * math.pi / latitudes)
    cosine_table = jnp.cos(angles)
    sine_table = jnp.sin(angles)
    forward = jnp.concatenate(
        [
            jnp.concatenate([cosine_table, sine_table], 1),
            jnp.concatenate([-sine_table, cosine_table], 1),
        ],
        0,
    )
    backward = jnp.concatenate(
        [
            jnp.concatenate([cosine_table, -sine_table], 1),
            jnp.concatenate([sine_table, cosine_table], 1),
        ],
        0,
    )
    return (forward, backward)


def mix_blocks(spectra, filters):
    extent = spectra.shape
    halves = spectra.reshape(extent[0], 2, extent[2], extent[3], filters.shape[2], filters.shape[3])
    nonimaginary_component = halves[:, 0]
    imag_part = halves[:, 1]

    def product(operand, matrix):
        return jnp.einsum("mhknb,nbc->mhknc", operand, matrix, precision=HIGHEST_PRECISION)

    first_real = jax.nn.relu(
        product(nonimaginary_component, filters[0, 0]) - product(imag_part, filters[0, 1])
    )
    first_imag = jax.nn.relu(
        product(nonimaginary_component, filters[0, 1]) + product(imag_part, filters[0, 0])
    )
    second_real = product(first_real, filters[1, 0]) - product(first_imag, filters[1, 1])
    second_imag = product(first_real, filters[1, 1]) + product(first_imag, filters[1, 0])
    blended = jnp.stack([second_real, second_imag], axis=1)
    blended = blended - jnp.clip(blended, -SHRINK_LEVEL, SHRINK_LEVEL)
    return blended.reshape(extent)


def spectral_filter(normed_one, filters, tables):
    forward, backward, lat_forward, lat_backward = tables
    spectra = jnp.einsum("rkw,mhwd->mrhkd", forward, normed_one, precision=HIGHEST_PRECISION)
    collected_fields = lax.all_to_all(spectra, "space", split_axis=3, concat_axis=2, tiled=True)
    extent = collected_fields.shape
    stacked = collected_fields.reshape(extent[0], 2 * extent[2], extent[3], extent[4])
    turned = jnp.einsum("ab,mbkd->makd", lat_forward, stacked, precision=HIGHEST_PRECISION)
    blended_modes = mix_blocks(turned.reshape(extent), filters).reshape(stacked.shape)
    inverse = jnp.einsum(
        "ab,mbkd->makd", lat_backward, blended_modes, precision=HIGHEST_PRECISION
    ).reshape(extent)
    returned = lax.all_to_all(inverse, "space", split_axis=2, concat_axis=3, tiled=True)
    return jnp.einsum("rkw,mrhkd->mhwd", backward, returned, precision=HIGHEST_PRECISION)


def on_device(
    state_in,
    member_ids,
    member_table,
    pos_embed,
    readout_tile_matrix,
    tile_lifting_matrix,
    norm_gain,
    norm_shift,
    spectral,
    up_weight,
    down_weight,
):
    position = lax.axis_index("segment")
    segment_count = lax.axis_size("segment")
    current = state_in[0, 0]
    channels = current.shape[3]
    latitudes = current.shape[1] * lax.axis_size("space")
    forward, backward = longitude_tables(current.shape[2], KW, latitudes)
    lat_forward, lat_backward = latitude_tables(latitudes)
    tables = (forward, backward, lat_forward, lat_backward)
    gains = norm_gain[0]
    shifts = norm_shift[0]
    filters = spectral[0]
    slot_index = -0 % segment_count
    chosen = member_ids[0, slot_index]
    onehot = (
        chosen[:, None] == jnp.arange(member_table.shape[0], dtype=jnp.int32)[None, :]
    ).astype(jnp.bfloat16)
    sample_trajectory_lines = jnp.dot(onehot, member_table, preferred_element_type=jnp.float32)

    def enter_grid(values):
        standardized_field = layer_norm(values.astype(jnp.float32)).astype(jnp.bfloat16)
        prediction_increment = jnp.einsum(
            "fbrd,do->fbro",
            standardized_field,
            readout_tile_matrix,
            preferred_element_type=jnp.float32,
        ).astype(jnp.bfloat16)
        admitted_lines = jnp.einsum(
            "nzwt,tl->nzwl",
            prediction_increment,
            tile_lifting_matrix,
            preferred_element_type=jnp.float32,
        )
        return (
            admitted_lines
            + pos_embed.astype(jnp.float32)[None]
            + sample_trajectory_lines[:, None, None, :]
        )

    def cast_values(values):
        return values.astype(jnp.float32)

    carried = lax.cond(position == 0, enter_grid, cast_values, current)
    normed_one = layer_norm(carried) * gains[0] + shifts[0]
    blended = carried + normed_one + spectral_filter(normed_one, filters, tables)
    normed_two = (layer_norm(blended) * gains[1] + shifts[1]).astype(jnp.bfloat16)
    flat_rows = normed_two.reshape(-1, channels)
    columns = flat_rows
    lifted = jnp.dot(
        columns,
        lax.all_gather(up_weight, ("space", "ens"), axis=1, tiled=True)[0],
        preferred_element_type=jnp.float32,
    )
    hidden = jax.nn.gelu(lifted, approximate=False).astype(jnp.bfloat16)
    columns = hidden
    update = jnp.dot(
        columns,
        lax.all_gather(down_weight, ("space", "ens"), axis=1, tiled=True)[0],
        preferred_element_type=jnp.float32,
    ).reshape(blended.shape)
    current = shifted((blended + update).astype(jnp.bfloat16), "segment", 1)
    return current[None, None]


ROW_STEP = 192
GROUP_LANES = 128
MESH_AXES = ("segment", "space", "ens")


def split_table(table):
    high = table.astype(ml_dtypes.bfloat16)
    low = (table - high.astype(np.float64)).astype(ml_dtypes.bfloat16)
    return np.stack([high, low])


def split_longitude_tables(longitudes, kept, latitudes):
    number = np.arange(kept)[:, None]
    points = np.arange(longitudes)[None, :]
    angles = (number * points % longitudes) * (2.0 * math.pi / longitudes)
    factor = 1.0 / math.sqrt(latitudes * longitudes)
    doubled = np.where(number == 0, 1.0, 2.0) * factor
    forward = np.concatenate([np.cos(angles) * factor, -np.sin(angles) * factor], 0)
    backward = np.concatenate([np.cos(angles) * doubled, -np.sin(angles) * doubled], 0).T
    return split_table(forward), split_table(backward)


def three_point(x, sign):
    (ar, ai), (br, bi), (cr, ci) = x
    tr, ti = br + cr, bi + ci
    mr, mi = ar - 0.5 * tr, ai - 0.5 * ti
    scale = math.sin(math.pi / 3.0) * sign
    dr, di = (br - cr) * scale, (bi - ci) * scale
    return [(ar + tr, ai + ti), (mr - di, mi + dr), (mr + di, mi - dr)]


def four_point(x, sign):
    (ar, ai), (br, bi), (cr, ci), (dr, di) = x
    sr, si, tr, ti = ar + cr, ai + ci, ar - cr, ai - ci
    ur, ui, vr, vi = br + dr, bi + di, br - dr, bi - di
    plus, minus = (tr - vi, ti + vr), (tr + vi, ti - vr)
    if sign < 0:
        plus, minus = minus, plus
    return [(sr + ur, si + ui), plus, (sr - ur, si - ui), minus]


def twelve_point(x, sign):
    columns = [three_point([x[(4 * a + 3 * b) % 12] for a in range(3)], sign) for b in range(4)]
    out = [None] * 12
    for a in range(3):
        line = four_point([columns[b][a] for b in range(4)], sign)
        for b in range(4):
            out[(4 * a + 9 * b) % 12] = line[b]
    return out


def lane_index(shape):
    return lax.broadcasted_iota(jnp.int32, shape, len(shape) - 1)


def spread_groups(values):
    a, b, c = (values[:, 128 * i : 128 * i + 128] for i in range(3))
    lanes = lane_index(a.shape)
    second = jnp.where(lanes < 32, pltpu.roll(a, 32, 1), pltpu.roll(b, 32, 1))
    third = jnp.where(lanes < 64, pltpu.roll(b, 64, 1), pltpu.roll(c, 64, 1))
    return jnp.concatenate([a, second, third, pltpu.roll(c, 96, 1)], 1)


def gather_groups(values):
    a, b, c, d = (values[:, 128 * i : 128 * i + 128] for i in range(4))
    lanes = lane_index(a.shape)
    first = jnp.where(lanes < 96, a, pltpu.roll(b, 96, 1))
    second = jnp.where(lanes < 64, pltpu.roll(b, 96, 1), pltpu.roll(c, 64, 1))
    third = jnp.where(lanes < 32, pltpu.roll(c, 64, 1), pltpu.roll(d, 32, 1))
    return jnp.concatenate([first, second, third], 1)


def gelu(x):
    return 0.5 * x * (1.0 + lax.erf(x * math.sqrt(0.5)))


def enter_kernel(
    scalars_ref,
    state_ref,
    readout_hbm,
    lifting_hbm,
    pos_hbm,
    table_hbm,
    out_ref,
    readout_ref,
    lifting_ref,
    pos_ref,
    table_ref,
    rows_ref,
    sems,
):
    first_segment, member = scalars_ref[0] == 0, scalars_ref[1]
    rows, width = state_ref.shape[:2]

    @pl.when(first_segment)
    def _():
        pairs = (
            (readout_hbm, readout_ref),
            (lifting_hbm, lifting_ref),
            (pos_hbm, pos_ref),
            (table_hbm, table_ref),
        )
        loads = [
            pltpu.make_async_copy(source, target, sems.at[number])
            for number, (source, target) in enumerate(pairs)
        ]
        for load in loads:
            load.start()
        rows_ref[...] = jnp.zeros_like(rows_ref)
        for row in range(rows):
            normed = layer_norm(state_ref[row].astype(jnp.float32)).astype(jnp.bfloat16)
            rows_ref[pl.ds(ROW_STEP * row, width)] = normed
        loads[0].wait()
        loads[3].wait()
        members = table_ref.shape[0]
        chosen = lax.broadcasted_iota(jnp.int32, (8, members), 1) == member
        line = jnp.dot(
            jnp.where(chosen, 1.0, 0.0).astype(jnp.bfloat16),
            table_ref[...],
            preferred_element_type=jnp.float32,
        )[0:1]
        for first in range(0, rows, 2):
            block = rows_ref[pl.ds(ROW_STEP * first, 2 * ROW_STEP)]
            forecast = jnp.dot(block, readout_ref[...], preferred_element_type=jnp.float32)
            if first == 0:
                loads[1].wait()
                loads[2].wait()
            lifted = jnp.dot(
                forecast.astype(jnp.bfloat16), lifting_ref[...], preferred_element_type=jnp.float32
            )
            for row in range(2):
                part = lifted[ROW_STEP * row : ROW_STEP * row + width]
                carried = part + pos_ref[first + row].astype(jnp.float32) + line
                out_ref[first + row] = carried.astype(jnp.bfloat16)

    @pl.when(jnp.logical_not(first_segment))
    def _():
        out_ref[...] = state_ref[...]


def filter_kernel(
    scalars_ref,
    entered_ref,
    moved_ref,
    near_state_ref,
    far_state_ref,
    norms_ref,
    taken_norms_ref,
    forward_ref,
    backward_ref,
    filters_hbm,
    taken_filters_hbm,
    out_ref,
    grid_ref,
    modes_ref,
    filters_ref,
    mixing_ref,
    own_ref,
    other_ref,
    sem,
    state_sems,
):
    half = scalars_ref[0]
    lower = half == 0
    rows = own_ref.shape[0]
    channels = own_ref.shape[2] // 2
    kept = grid_ref.shape[1] // 2
    groups = modes_ref.shape[0]
    side = filters_ref.shape[-1]
    near = half == scalars_ref[1]
    state_loads = start_loads(
        near,
        [entered_ref, far_state_ref],
        [moved_ref, near_state_ref],
        [own_ref, other_ref],
        state_sems,
    )
    wanted = pl.ds(half * groups, groups)
    own_load = pltpu.make_async_copy(filters_hbm.at[:, :, wanted], filters_ref, sem)
    taken_load = pltpu.make_async_copy(taken_filters_hbm.at[:, :, wanted], filters_ref, sem)
    pl.when(near)(own_load.start)
    pl.when(jnp.logical_not(near))(taken_load.start)
    norms = jnp.where(near, norms_ref[...], taken_norms_ref[...])
    bases = (half * rows, (1 - half) * rows)

    def dot(a, b):
        return jnp.dot(a, b, preferred_element_type=jnp.float32)

    def chosen(values):
        return jnp.where(lower, values[:, :channels], values[:, channels:])

    gain, shift = chosen(norms[0:1]), chosen(norms[2:3])
    for row in range(rows):
        for source, base, load in zip((own_ref, other_ref), bases, state_loads):
            if row == 0:
                load.wait()
            values = source[row].astype(jnp.float32)
            average = jnp.mean(values, axis=-1, keepdims=True)
            centred = values - average
            spread = jnp.mean(centred * centred, axis=-1, keepdims=True)
            normed = chosen(centred) * lax.rsqrt(spread + EPSILON) * gain + shift
            points = spread_groups(normed).astype(jnp.bfloat16)
            grid_ref[base + row] = dot(forward_ref[0], points) + dot(forward_ref[1], points)

    mixing_ref[...] = jnp.zeros_like(mixing_ref)
    own_load.wait()
    first, second = pl.ds(0, side), pl.ds(GROUP_LANES, side)
    for layer in range(2):
        for group in range(groups):
            real = filters_ref[layer, 0, group].astype(jnp.bfloat16)
            imag = filters_ref[layer, 1, group].astype(jnp.bfloat16)
            mixing_ref[layer, group, first, first] = real
            mixing_ref[layer, group, first, second] = imag
            mixing_ref[layer, group, second, first] = -imag
            mixing_ref[layer, group, second, second] = real

    def turn(step, carry):
        low = pl.multiple_of(step * 8, 8)
        for group in range(groups):
            lanes = pl.ds(GROUP_LANES * group, GROUP_LANES)
            values = [
                (grid_ref[h, pl.ds(low, 8), lanes], grid_ref[h, pl.ds(kept + low, 8), lanes])
                for h in range(12)
            ]
            for k, (real, imag) in enumerate(twelve_point(values, -1)):
                at = pl.ds(k * kept + low, 8)
                modes_ref[group, at, pl.ds(0, GROUP_LANES)] = real
                modes_ref[group, at, pl.ds(GROUP_LANES, GROUP_LANES)] = imag
        return carry

    lax.fori_loop(0, kept // 8, turn, 0)
    for group in range(groups):
        u = jax.nn.relu(dot(modes_ref[group].astype(jnp.bfloat16), mixing_ref[0, group]))
        v = dot(u.astype(jnp.bfloat16), mixing_ref[1, group])
        modes_ref[group] = v - jnp.clip(v, -SHRINK_LEVEL, SHRINK_LEVEL)

    def turn_back(step, carry):
        low = pl.multiple_of(step * 8, 8)
        for group in range(groups):
            lanes = pl.ds(GROUP_LANES * group, GROUP_LANES)
            values = []
            for k in range(12):
                at = pl.ds(k * kept + low, 8)
                values.append(
                    (
                        modes_ref[group, at, pl.ds(0, GROUP_LANES)],
                        modes_ref[group, at, pl.ds(GROUP_LANES, GROUP_LANES)],
                    )
                )
            for h, (real, imag) in enumerate(twelve_point(values, 1)):
                grid_ref[h, pl.ds(low, 8), lanes] = real
                grid_ref[h, pl.ds(kept + low, 8), lanes] = imag
        return carry

    lax.fori_loop(0, kept // 8, turn_back, 0)
    for part, base in enumerate(bases):
        for row in range(rows):
            spectra = grid_ref[base + row].astype(jnp.bfloat16)
            filtered = dot(backward_ref[0], spectra) + dot(backward_ref[1], spectra)
            out_ref[part * rows + row] = gather_groups(filtered).astype(out_ref.dtype)


def start_loads(near, near_refs, far_refs, targets, sems):
    def copies(refs):
        return [
            pltpu.make_async_copy(ref, target, sems.at[number])
            for number, (ref, target) in enumerate(zip(refs, targets))
        ]

    @pl.when(near)
    def _():
        for copy in copies(near_refs):
            copy.start()

    @pl.when(jnp.logical_not(near))
    def _():
        for copy in copies(far_refs):
            copy.start()

    return copies(near_refs)


def hidden_kernel(
    count,
    scalars_ref,
    entered_ref,
    moved_ref,
    near_state_ref,
    far_state_ref,
    mine_ref,
    theirs_ref,
    norms_ref,
    taken_norms_ref,
    held_ref,
    first_ref,
    second_ref,
    third_ref,
    relayed_ref,
    blended_ref,
    hidden_ref,
    rows_ref,
    up_ref,
    own_ref,
    other_ref,
    sems,
    state_sems,
):
    half, space, member = scalars_ref[0], scalars_ref[1], scalars_ref[2]
    rows, width, channels = own_ref.shape
    state_loads = start_loads(
        half == space,
        [entered_ref, far_state_ref],
        [moved_ref, near_state_ref],
        [own_ref, other_ref],
        state_sems,
    )
    depth = held_ref.shape[0]
    here, away = 2 * space, 2 * (1 - space)
    order = [here + member, here + 1 - member, away + member, away + 1 - member]
    loads = start_loads(
        half == space,
        [held_ref, first_ref, second_ref, relayed_ref],
        [second_ref, third_ref, first_ref, relayed_ref],
        [up_ref.at[pl.ds(pl.multiple_of(shard * depth, depth), depth)] for shard in order],
        sems,
    )
    rows_ref[...] = jnp.zeros_like(rows_ref)
    norms = jnp.where(half == space, norms_ref[...], taken_norms_ref[...])

    def enter_rows(part, row):
        source = (own_ref, other_ref)[part]
        carried = source[row].astype(jnp.float32)
        normed = layer_norm(carried) * norms[0:1] + norms[2:3]
        mine = mine_ref[part * rows + row].astype(jnp.float32)
        theirs = theirs_ref[(1 - part) * rows + row].astype(jnp.float32)
        low = jnp.where(half == 0, mine, theirs)
        high = jnp.where(half == 0, theirs, mine)
        blended = carried + normed + jnp.concatenate([low, high], 1)
        if part == 0:
            blended_ref[row] = blended
        again = layer_norm(blended) * norms[1:2] + norms[3:4]
        place = row // count * 2 * count + part * count + row % count
        rows_ref[pl.ds(ROW_STEP * place, width)] = again.astype(jnp.bfloat16)

    for load in state_loads:
        load.wait()
    step = up_ref.shape[1] // 2
    for block in range(rows // count):
        for part in range(2):
            for row in range(count):
                enter_rows(part, count * block + row)
        if block == 0:
            for copy in loads:
                copy.wait()
        at = pl.ds(2 * count * ROW_STEP * block, 2 * count * ROW_STEP)
        values = rows_ref[at]
        for column in range(0, up_ref.shape[1], step):
            lifted = jnp.dot(
                values, up_ref[:, pl.ds(column, step)], preferred_element_type=jnp.float32
            )
            hidden_ref[at, pl.ds(column, step)] = gelu(lifted).astype(jnp.bfloat16)


def update_kernel(
    number,
    scalars_ref,
    blended_ref,
    hidden_ref,
    held_ref,
    near_ref,
    far_ref,
    relayed_ref,
    own_ref,
    other_ref,
    down_ref,
    sems,
):
    half, space, member = scalars_ref[0], scalars_ref[1], scalars_ref[2]
    count, width, channels = own_ref.shape
    depth = held_ref.shape[0]
    loads = start_loads(
        half == space,
        [held_ref, near_ref],
        [far_ref, relayed_ref],
        [
            down_ref.at[pl.ds(pl.multiple_of(shard * depth, depth), depth)]
            for shard in (member, 1 - member)
        ],
        sems,
    )
    rows_here = pl.ds(2 * count * ROW_STEP * number, 2 * count * ROW_STEP)
    update = None
    for copy, shard in zip(loads, (member, 1 - member)):
        copy.wait()
        at = pl.ds(pl.multiple_of(shard * depth, depth), depth)
        more = jnp.dot(
            hidden_ref[rows_here, at], down_ref[at], preferred_element_type=jnp.float32
        )
        update = more if update is None else update + more
    for row in range(count):
        part = update[ROW_STEP * row : ROW_STEP * row + width]
        own_ref[row] = blended_ref[count * number + row] + part
        part = update[ROW_STEP * (count + row) : ROW_STEP * (count + row) + width]
        other_ref[row] = part.astype(other_ref.dtype)


def place_kernel(start, chunk_ref, out_ref, sem):
    copy = pltpu.make_async_copy(chunk_ref, out_ref.at[pl.ds(start, chunk_ref.shape[0])], sem)
    copy.start()
    copy.wait()


def collect_kernel(relayed_ref, *refs):
    sources, out_ref, sems = refs[:-3], refs[-2], refs[-1]
    parts = len(sources) // 2
    count = sources[0].shape[0]

    def copies(step):
        return [
            pltpu.make_async_copy(
                sources[2 * part + step],
                out_ref.at[pl.ds(count * part, count)],
                sems.at[part],
            )
            for part in range(parts)
        ]

    for step in range(2):

        @pl.when(relayed_ref[0] == step)
        def _():
            for copy in copies(step):
                copy.start()

    for copy in copies(0):
        copy.wait()


VMEM = pltpu.VMEM
SCALARS = pl.BlockSpec(memory_space=pltpu.SMEM)
WHOLE = pl.BlockSpec(memory_space=pltpu.VMEM)
LEFT = pl.BlockSpec(memory_space=pltpu.HBM)


def cost(microseconds):
    return pl.CostEstimate(
        flops=int(microseconds * 2e8), bytes_accessed=0, transcendentals=0
    )


def params(megabytes):
    return pltpu.CompilerParams(vmem_limit_bytes=megabytes * 2**20)


def fast_on_device(
    sizes,
    state_in,
    member_ids,
    member_table,
    pos_embed,
    readout_tile_matrix,
    tile_lifting_matrix,
    norm_gain,
    norm_shift,
    spectral,
    up_weight,
    down_weight,
):
    segments, spaces, members = sizes
    position = lax.axis_index("segment")
    core = position % 2
    space = lax.axis_index("space")
    member = lax.axis_index("ens")
    near = core == space

    def table(target):
        pairs = []
        for g in range(segments):
            for s in range(spaces):
                for e in range(members):
                    to = target(g, s, e)
                    if to is not None:
                        flat = (to[0] * spaces + to[1]) * members + to[2]
                        pairs.append(((g * spaces + s) * members + e, flat))
        return pairs

    def send(value, pairs):
        return lax.ppermute(value, MESH_AXES, pairs)

    def keeps(g, s):
        return g % 2 == s

    def moved_place(g, s, e):
        return (g // 2 * 2 + s, g % 2, e)

    far_relocate = table(lambda g, s, e: None if keeps(g, s) else moved_place(g, s, e))
    first_way = table(lambda g, s, e: (g, s, 1 - e) if keeps(g, s) else moved_place(g, s, e))
    second_way = table(lambda g, s, e: (g ^ 1, s, e) if keeps(g, s) else (g, 1 - s, e))
    near_across = table(lambda g, s, e: (g, s, 1 - e) if keeps(g, s) else None)
    across = table(lambda g, s, e: (g, s, 1 - e))
    third_way = table(lambda g, s, e: (g ^ 1, s, 1 - e) if keeps(g, s) else None)
    far_across = table(lambda g, s, e: (g, s, 1 - e) if not keeps(g, s) else None)
    far_to_other = table(lambda g, s, e: (g ^ 1, s, e) if not keeps(g, s) else None)
    swap_cores = table(lambda g, s, e: (g ^ 1, s, e))
    near_to_other = table(lambda g, s, e: (g ^ 1, s, e) if keeps(g, s) else None)
    onward = table(lambda g, s, e: ((g // 2 * 2 + s + 1) % segments, g % 2, e))
    onward_by_space = table(
        lambda g, s, e: (g, 0, e)
        if s == 1 and g % 2 == 0
        else ((g // 2 * 2 + s + 1) % segments, g % 2, e)
    )
    onward_rest = table(
        lambda g, s, e: ((g + 2) % segments, 0, e) if s == 0 and g % 2 == 0 else None
    )

    state = state_in[0, 0, 0]
    rows, width, channels = state.shape
    latitudes = rows * spaces
    bf16, f32, i32 = jnp.bfloat16, jnp.float32, jnp.int32
    up, down = up_weight[0], down_weight[0]
    hidden_half = up.shape[1] // 2
    scalars = jnp.stack([core, space, member]).astype(i32)

    up_held = lax.dynamic_slice_in_dim(up, space * hidden_half, hidden_half, 1)
    up_held, up_again = lax.optimization_barrier((up_held, up))
    up_given = lax.dynamic_slice_in_dim(up_again, (1 - space) * hidden_half, hidden_half, 1)
    up_first = send(up_held, first_way)
    up_second = send(up_given, second_way)
    entered = pl.pallas_call(
        enter_kernel,
        out_shape=VMEM(state.shape, bf16),
        in_specs=[SCALARS, WHOLE] + [LEFT] * 4,
        out_specs=WHOLE,
        scratch_shapes=[
            VMEM(readout_tile_matrix.shape, bf16),
            VMEM(tile_lifting_matrix.shape, bf16),
            VMEM(pos_embed.shape, bf16),
            VMEM(member_table.shape, bf16),
            VMEM((rows * ROW_STEP, channels), bf16),
            pltpu.SemaphoreType.DMA((4,)),
        ],
        cost_estimate=cost(9),
        compiler_params=params(58),
    )(
        jnp.stack([position, member_ids[0, 0, 0]]).astype(i32),
        state,
        readout_tile_matrix,
        tile_lifting_matrix,
        pos_embed,
        member_table,
    )
    up_third = send(up_given, third_way)
    entered, up_first, up_second, up_third = lax.optimization_barrier(
        (entered, up_first, up_second, up_third)
    )
    moved = send(entered, far_relocate)
    near_state = send(entered, near_to_other)
    up_relayed = send(jnp.where(near, up_second, up_first), across)
    norms = jnp.concatenate([norm_gain[0], norm_shift[0]], 0)
    taken_norms = send(norms, near_to_other)
    filters = spectral[0]
    taken_filters = send(filters, near_to_other)
    moved, near_state, up_relayed, taken_norms, taken_filters, down_later = (
        lax.optimization_barrier(
            (moved, near_state, up_relayed, taken_norms, taken_filters, down)
        )
    )
    far_state = send(moved, far_to_other)
    down_far = send(down_later, far_relocate)
    down_near = send(down_later, near_across)
    states = (entered, moved, near_state, far_state)

    forward, backward = split_longitude_tables(width, KW, latitudes)
    half_groups = spectral.shape[3] // 2
    lanes = half_groups * GROUP_LANES
    filtered = pl.pallas_call(
        filter_kernel,
        out_shape=jax.ShapeDtypeStruct((2 * rows, width, channels // 2), bf16),
        in_specs=[SCALARS] + [LEFT] * 4 + [WHOLE] * 4 + [LEFT] * 2,
        out_specs=WHOLE,
        scratch_shapes=[
            VMEM((latitudes, 2 * KW, lanes), f32),
            VMEM((half_groups, latitudes * KW, 2 * GROUP_LANES), f32),
            VMEM((2, 2, half_groups) + filters.shape[3:], f32),
            VMEM((2, half_groups, 2 * GROUP_LANES, 2 * GROUP_LANES), bf16),
            VMEM(state.shape, bf16),
            VMEM(state.shape, bf16),
            pltpu.SemaphoreType.DMA,
            pltpu.SemaphoreType.DMA((2,)),
        ],
        cost_estimate=cost(11),
        compiler_params=params(24),
    )(
        scalars,
        *states,
        norms,
        taken_norms,
        jnp.asarray(forward),
        jnp.asarray(backward),
        filters,
        taken_filters,
    )
    filtered, down_far, down_near = lax.optimization_barrier((filtered, down_far, down_near))
    down_relayed = send(down_far, far_across)
    filtered_other = send(filtered, swap_cores)

    parts = 2
    blended, hidden = pl.pallas_call(
        functools.partial(hidden_kernel, rows // parts),
        out_shape=[
            VMEM(state.shape, f32),
            VMEM((2 * rows * ROW_STEP, hidden_half), bf16),
        ],
        in_specs=[SCALARS] + [LEFT] * 4 + [WHOLE] * 4 + [LEFT] * 5,
        out_specs=[WHOLE] * 2,
        scratch_shapes=[
            VMEM((2 * rows * ROW_STEP, channels), bf16),
            VMEM((channels, hidden_half), bf16),
            VMEM(state.shape, bf16),
            VMEM(state.shape, bf16),
            pltpu.SemaphoreType.DMA((4,)),
            pltpu.SemaphoreType.DMA((2,)),
        ],
        cost_estimate=cost(11),
        compiler_params=params(30),
    )(
        scalars,
        *states,
        filtered,
        filtered_other,
        norms,
        taken_norms,
        up_held,
        up_first,
        up_second,
        up_third,
        up_relayed,
    )
    landed, ready = [], []
    for number in range(parts):
        own, other = pl.pallas_call(
            functools.partial(update_kernel, number),
            out_shape=[
                jax.ShapeDtypeStruct((rows // parts, width, channels), f32),
                jax.ShapeDtypeStruct((rows // parts, width, channels), bf16),
            ],
            in_specs=[SCALARS] + [WHOLE] * 2 + [LEFT] * 4,
            out_specs=[WHOLE] * 2,
            scratch_shapes=[
                VMEM((2 * hidden_half // 2, channels), bf16),
                pltpu.SemaphoreType.DMA((2,)),
            ],
            cost_estimate=cost(50),
            compiler_params=params(24),
        )(scalars, blended, hidden, down, down_near, down_far, down_relayed)
        ready.append((own + send(other, swap_cores).astype(f32)).astype(bf16))
        if number + 1 < parts:
            landed.append([send(ready[-1], onward_by_space)])
        else:
            landed.append([send(ready[-1], onward)])
    for number in range(parts - 1):
        first_hop = landed[number][0]
        if number > 0:
            first_hop, _ = lax.optimization_barrier((first_hop, ready[-1]))
        landed[number].append(send(first_hop, onward_rest))
    relayed = (core + space == 0).astype(i32)[None]
    out = pl.pallas_call(
        functools.partial(place_kernel, rows // parts * (parts - 1)),
        out_shape=jax.ShapeDtypeStruct(state.shape, bf16),
        in_specs=[WHOLE],
        out_specs=LEFT,
        scratch_shapes=[pltpu.SemaphoreType.DMA],
        cost_estimate=cost(100),
        compiler_params=params(16),
    )(landed[-1][0])
    arrived = [value for chunk in landed[:-1] for value in chunk]
    out = pl.pallas_call(
        collect_kernel,
        out_shape=jax.ShapeDtypeStruct(state.shape, bf16),
        in_specs=[SCALARS] + [WHOLE] * len(arrived) + [LEFT],
        out_specs=LEFT,
        input_output_aliases={1 + len(arrived): 0},
        scratch_shapes=[pltpu.SemaphoreType.DMA((parts - 1,))],
        compiler_params=params(16),
    )(relayed, *arrived, out)
    return out[None, None, None]


def solution(mesh):
    placed = (
        P("ens", "segment", None, "space", None, None),
        P("ens", None, None),
        P(),
        P("space", None, None),
        P(),
        P(),
        P("segment", None, None),
        P("segment", None, None),
        P("segment", None, None, None, None, None),
        P("segment", ("space", "ens"), None),
        P("segment", ("space", "ens"), None),
    )
    sizes = tuple(mesh.shape[axis] for axis in MESH_AXES)
    whole_micro_batch_on_a_chip = sizes[0] % 2 == 0 and sizes[1:] == (2, 2)
    if whole_micro_batch_on_a_chip:
        program = functools.partial(fast_on_device, sizes)
    else:
        program = on_device
    return jax.shard_map(
        program,
        mesh=mesh,
        in_specs=placed,
        out_specs=P("ens", "segment", None, "space", None, None),
        check_vma=False,
    )
```

```python
import functools
import math

import jax
import jax.numpy as jnp
import ml_dtypes
import numpy as np
from jax import lax
from jax.experimental import pallas as pl
from jax.experimental.pallas import tpu as pltpu
from jax.sharding import PartitionSpec as P

KW = 88


EPSILON = 1e-05
SHRINK_LEVEL = 0.01
HIGHEST_PRECISION = lax.Precision.HIGHEST


def shifted(value, axis, steps):
    count = lax.axis_size(axis)
    pairs = [(source, (source + steps) % count) for source in range(count)]
    return lax.ppermute(value, axis, pairs)


def layer_norm(values):
    average = jnp.mean(values, axis=-1, keepdims=True)
    centred = values - average
    spread = jnp.mean(centred * centred, axis=-1, keepdims=True)
    return centred * lax.rsqrt(spread + EPSILON)


def longitude_tables(longitudes, kept, latitudes):
    number = jnp.arange(kept, dtype=jnp.int32)[:, None]
    points = jnp.arange(longitudes, dtype=jnp.int32)[None, :]
    angles = (number * points % longitudes).astype(jnp.float32) * (2.0 * math.pi / longitudes)
    factor = 1.0 / math.sqrt(latitudes * longitudes)
    doubled = jnp.where(number == 0, 1.0, 2.0).astype(jnp.float32) * factor
    forward = jnp.stack([jnp.cos(angles) * factor, -jnp.sin(angles) * factor])
    backward = jnp.stack([jnp.cos(angles) * doubled, -jnp.sin(angles) * doubled])
    return (forward, backward)


def latitude_tables(latitudes):
    number = jnp.arange(latitudes, dtype=jnp.int32)[:, None]
    points = jnp.arange(latitudes, dtype=jnp.int32)[None, :]
    angles = (number * points % latitudes).astype(jnp.float32) * (2.0 * math.pi / latitudes)
    cosine_table = jnp.cos(angles)
    sine_table = jnp.sin(angles)
    forward = jnp.concatenate(
        [
            jnp.concatenate([cosine_table, sine_table], 1),
            jnp.concatenate([-sine_table, cosine_table], 1),
        ],
        0,
    )
    backward = jnp.concatenate(
        [
            jnp.concatenate([cosine_table, -sine_table], 1),
            jnp.concatenate([sine_table, cosine_table], 1),
        ],
        0,
    )
    return (forward, backward)


def mix_blocks(spectra, filters):
    extent = spectra.shape
    halves = spectra.reshape(extent[0], 2, extent[2], extent[3], filters.shape[2], filters.shape[3])
    nonimaginary_component = halves[:, 0]
    imag_part = halves[:, 1]

    def product(operand, matrix):
        return jnp.einsum("mhknb,nbc->mhknc", operand, matrix, precision=HIGHEST_PRECISION)

    first_real = jax.nn.relu(
        product(nonimaginary_component, filters[0, 0]) - product(imag_part, filters[0, 1])
    )
    first_imag = jax.nn.relu(
        product(nonimaginary_component, filters[0, 1]) + product(imag_part, filters[0, 0])
    )
    second_real = product(first_real, filters[1, 0]) - product(first_imag, filters[1, 1])
    second_imag = product(first_real, filters[1, 1]) + product(first_imag, filters[1, 0])
    blended = jnp.stack([second_real, second_imag], axis=1)
    blended = blended - jnp.clip(blended, -SHRINK_LEVEL, SHRINK_LEVEL)
    return blended.reshape(extent)


def spectral_filter(normed_one, filters, tables):
    forward, backward, lat_forward, lat_backward = tables
    spectra = jnp.einsum("rkw,mhwd->mrhkd", forward, normed_one, precision=HIGHEST_PRECISION)
    collected_fields = lax.all_to_all(spectra, "space", split_axis=3, concat_axis=2, tiled=True)
    extent = collected_fields.shape
    stacked = collected_fields.reshape(extent[0], 2 * extent[2], extent[3], extent[4])
    turned = jnp.einsum("ab,mbkd->makd", lat_forward, stacked, precision=HIGHEST_PRECISION)
    blended_modes = mix_blocks(turned.reshape(extent), filters).reshape(stacked.shape)
    inverse = jnp.einsum(
        "ab,mbkd->makd", lat_backward, blended_modes, precision=HIGHEST_PRECISION
    ).reshape(extent)
    returned = lax.all_to_all(inverse, "space", split_axis=2, concat_axis=3, tiled=True)
    return jnp.einsum("rkw,mrhkd->mhwd", backward, returned, precision=HIGHEST_PRECISION)


def on_device(
    state_in,
    member_ids,
    member_table,
    pos_embed,
    readout_tile_matrix,
    tile_lifting_matrix,
    norm_gain,
    norm_shift,
    spectral,
    up_weight,
    down_weight,
):
    position = lax.axis_index("segment")
    segment_count = lax.axis_size("segment")
    current = state_in[0, 0]
    channels = current.shape[3]
    latitudes = current.shape[1] * lax.axis_size("space")
    forward, backward = longitude_tables(current.shape[2], KW, latitudes)
    lat_forward, lat_backward = latitude_tables(latitudes)
    tables = (forward, backward, lat_forward, lat_backward)
    gains = norm_gain[0]
    shifts = norm_shift[0]
    filters = spectral[0]
    slot_index = -0 % segment_count
    chosen = member_ids[0, slot_index]
    onehot = (
        chosen[:, None] == jnp.arange(member_table.shape[0], dtype=jnp.int32)[None, :]
    ).astype(jnp.bfloat16)
    sample_trajectory_lines = jnp.dot(onehot, member_table, preferred_element_type=jnp.float32)

    def enter_grid(values):
        standardized_field = layer_norm(values.astype(jnp.float32)).astype(jnp.bfloat16)
        prediction_increment = jnp.einsum(
            "fbrd,do->fbro",
            standardized_field,
            readout_tile_matrix,
            preferred_element_type=jnp.float32,
        ).astype(jnp.bfloat16)
        admitted_lines = jnp.einsum(
            "nzwt,tl->nzwl",
            prediction_increment,
            tile_lifting_matrix,
            preferred_element_type=jnp.float32,
        )
        return (
            admitted_lines
            + pos_embed.astype(jnp.float32)[None]
            + sample_trajectory_lines[:, None, None, :]
        )

    def cast_values(values):
        return values.astype(jnp.float32)

    carried = lax.cond(position == 0, enter_grid, cast_values, current)
    normed_one = layer_norm(carried) * gains[0] + shifts[0]
    blended = carried + normed_one + spectral_filter(normed_one, filters, tables)
    normed_two = (layer_norm(blended) * gains[1] + shifts[1]).astype(jnp.bfloat16)
    flat_rows = normed_two.reshape(-1, channels)
    columns = flat_rows
    lifted = jnp.dot(
        columns,
        lax.all_gather(up_weight, ("space", "ens"), axis=1, tiled=True)[0],
        preferred_element_type=jnp.float32,
    )
    hidden = jax.nn.gelu(lifted, approximate=False).astype(jnp.bfloat16)
    columns = hidden
    update = jnp.dot(
        columns,
        lax.all_gather(down_weight, ("space", "ens"), axis=1, tiled=True)[0],
        preferred_element_type=jnp.float32,
    ).reshape(blended.shape)
    current = shifted((blended + update).astype(jnp.bfloat16), "segment", 1)
    return current[None, None]


ROW_STEP = 192
GROUP_LANES = 128
MESH_AXES = ("segment", "space", "ens")


def split_table(table):
    high = table.astype(ml_dtypes.bfloat16)
    low = (table - high.astype(np.float64)).astype(ml_dtypes.bfloat16)
    return np.stack([high, low])


def split_longitude_tables(longitudes, kept, latitudes):
    number = np.arange(kept)[:, None]
    points = np.arange(longitudes)[None, :]
    angles = (number * points % longitudes) * (2.0 * math.pi / longitudes)
    factor = 1.0 / math.sqrt(latitudes * longitudes)
    doubled = np.where(number == 0, 1.0, 2.0) * factor
    forward = np.concatenate([np.cos(angles) * factor, -np.sin(angles) * factor], 0)
    backward = np.concatenate([np.cos(angles) * doubled, -np.sin(angles) * doubled], 0).T
    size = max(forward.shape)
    both = np.zeros((2, size, size))
    both[0, : forward.shape[0], : forward.shape[1]] = forward
    both[1, : backward.shape[0], : backward.shape[1]] = backward
    return split_table(both)


def three_point(x, sign):
    (ar, ai), (br, bi), (cr, ci) = x
    tr, ti = br + cr, bi + ci
    mr, mi = ar - 0.5 * tr, ai - 0.5 * ti
    scale = math.sin(math.pi / 3.0) * sign
    dr, di = (br - cr) * scale, (bi - ci) * scale
    return [(ar + tr, ai + ti), (mr - di, mi + dr), (mr + di, mi - dr)]


def four_point(x, sign):
    (ar, ai), (br, bi), (cr, ci), (dr, di) = x
    sr, si, tr, ti = ar + cr, ai + ci, ar - cr, ai - ci
    ur, ui, vr, vi = br + dr, bi + di, br - dr, bi - di
    plus, minus = (tr - vi, ti + vr), (tr + vi, ti - vr)
    if sign < 0:
        plus, minus = minus, plus
    return [(sr + ur, si + ui), plus, (sr - ur, si - ui), minus]


def twelve_point(x, sign):
    columns = [three_point([x[(4 * a + 3 * b) % 12] for a in range(3)], sign) for b in range(4)]
    out = [None] * 12
    for a in range(3):
        line = four_point([columns[b][a] for b in range(4)], sign)
        for b in range(4):
            out[(4 * a + 9 * b) % 12] = line[b]
    return out


def lane_index(shape):
    return lax.broadcasted_iota(jnp.int32, shape, len(shape) - 1)


def spread_groups(values):
    a, b, c = (values[:, 128 * i : 128 * i + 128] for i in range(3))
    lanes = lane_index(a.shape)
    second = jnp.where(lanes < 32, pltpu.roll(a, 32, 1), pltpu.roll(b, 32, 1))
    third = jnp.where(lanes < 64, pltpu.roll(b, 64, 1), pltpu.roll(c, 64, 1))
    return jnp.concatenate([a, second, third, pltpu.roll(c, 96, 1)], 1)


def gather_groups(values):
    a, b, c, d = (values[:, 128 * i : 128 * i + 128] for i in range(4))
    lanes = lane_index(a.shape)
    first = jnp.where(lanes < 96, a, pltpu.roll(b, 96, 1))
    second = jnp.where(lanes < 64, pltpu.roll(b, 96, 1), pltpu.roll(c, 64, 1))
    third = jnp.where(lanes < 32, pltpu.roll(c, 64, 1), pltpu.roll(d, 32, 1))
    return jnp.concatenate([first, second, third], 1)


def gelu(x):
    return 0.5 * x * (1.0 + lax.erf(x * math.sqrt(0.5)))


def enter_kernel(
    scalars_ref,
    state_ref,
    readout_hbm,
    lifting_hbm,
    pos_hbm,
    table_hbm,
    out_ref,
    readout_ref,
    lifting_ref,
    pos_ref,
    table_ref,
    rows_ref,
    sems,
):
    first_segment, member = scalars_ref[0] == 0, scalars_ref[1]
    rows, width = state_ref.shape[:2]

    @pl.when(first_segment)
    def _():
        pairs = (
            (readout_hbm, readout_ref),
            (lifting_hbm, lifting_ref),
            (pos_hbm, pos_ref),
            (table_hbm, table_ref),
        )
        loads = [
            pltpu.make_async_copy(source, target, sems.at[number])
            for number, (source, target) in enumerate(pairs)
        ]
        for load in loads:
            load.start()
        rows_ref[...] = jnp.zeros_like(rows_ref)
        for row in range(rows):
            normed = layer_norm(state_ref[row].astype(jnp.float32)).astype(jnp.bfloat16)
            rows_ref[pl.ds(ROW_STEP * row, width)] = normed
        loads[0].wait()
        loads[3].wait()
        members = table_ref.shape[0]
        chosen = lax.broadcasted_iota(jnp.int32, (8, members), 1) == member
        line = jnp.dot(
            jnp.where(chosen, 1.0, 0.0).astype(jnp.bfloat16),
            table_ref[...],
            preferred_element_type=jnp.float32,
        )[0:1]
        for first in range(0, rows, 2):
            block = rows_ref[pl.ds(ROW_STEP * first, 2 * ROW_STEP)]
            forecast = jnp.dot(block, readout_ref[...], preferred_element_type=jnp.float32)
            if first == 0:
                loads[1].wait()
                loads[2].wait()
            lifted = jnp.dot(
                forecast.astype(jnp.bfloat16), lifting_ref[...], preferred_element_type=jnp.float32
            )
            for row in range(2):
                part = lifted[ROW_STEP * row : ROW_STEP * row + width]
                carried = part + pos_ref[first + row].astype(jnp.float32) + line
                out_ref[first + row] = carried.astype(jnp.bfloat16)

    @pl.when(jnp.logical_not(first_segment))
    def _():
        out_ref[...] = state_ref[...]


def load_one(near, near_ref, far_ref, target, sem):
    near_copy = pltpu.make_async_copy(near_ref, target, sem)
    far_copy = pltpu.make_async_copy(far_ref, target, sem)
    pl.when(near)(near_copy.start)
    pl.when(jnp.logical_not(near))(far_copy.start)
    return near_copy


def centre(values):
    average = jnp.mean(values, axis=-1, keepdims=True)
    centred = values - average
    spread = jnp.mean(centred * centred, axis=-1, keepdims=True)
    return centred, lax.rsqrt(spread + EPSILON)


def dot(a, b):
    return jnp.dot(a, b, preferred_element_type=jnp.float32)


def row_spectra(lower, centred, factor, norms, forward):
    channels = centred.shape[1] // 2

    def chosen(values):
        return jnp.where(lower, values[:, :channels], values[:, channels:])

    normed = chosen(centred) * factor * chosen(norms[0:1]) + chosen(norms[2:3])
    points = spread_groups(normed).astype(jnp.bfloat16)
    return dot(forward[0], points) + dot(forward[1], points)


def near_kernel(
    scalars_ref,
    entered_ref,
    near_state_ref,
    norms_ref,
    taken_norms_ref,
    tables_ref,
    grid_ref,
    base_ref,
    state_ref,
    sem,
):
    half, space = scalars_ref[0], scalars_ref[1]
    near = half == space
    load = load_one(near, entered_ref, near_state_ref, state_ref, sem)
    rows, width, _ = state_ref.shape
    norms = jnp.where(near, norms_ref[...], taken_norms_ref[...])
    forward = [tables_ref[part, 0, : grid_ref.shape[1], :width] for part in range(2)]
    load.wait()
    for row in range(rows):
        carried = state_ref[row].astype(jnp.float32)
        centred, factor = centre(carried)
        base_ref[row] = carried + (centred * factor * norms[0:1] + norms[2:3])
        grid_ref[row] = row_spectra(half == 0, centred, factor, norms, forward)


def base_kernel(
    scalars_ref, moved_ref, far_state_ref, norms_ref, taken_norms_ref, base_ref, state_ref, sem
):
    near = scalars_ref[0] == scalars_ref[1]
    load = load_one(near, far_state_ref, moved_ref, state_ref, sem)
    norms = jnp.where(near, norms_ref[...], taken_norms_ref[...])
    load.wait()
    for row in range(state_ref.shape[0]):
        carried = state_ref[row].astype(jnp.float32)
        centred, factor = centre(carried)
        base_ref[row] = carried + (centred * factor * norms[0:1] + norms[2:3])


def filter_kernel(
    scalars_ref,
    moved_ref,
    far_state_ref,
    norms_ref,
    taken_norms_ref,
    tables_ref,
    near_grid_ref,
    filters_hbm,
    taken_filters_hbm,
    out_ref,
    grid_ref,
    modes_ref,
    filters_ref,
    mixing_ref,
    state_ref,
    sem,
    state_sem,
):
    half, space = scalars_ref[0], scalars_ref[1]
    near = half == space
    load = load_one(near, far_state_ref, moved_ref, state_ref, state_sem)
    rows, width, _ = state_ref.shape
    kept = grid_ref.shape[1] // 2
    groups = modes_ref.shape[0]
    side = filters_ref.shape[-1]
    wanted = pl.ds(half * groups, groups)
    own_load = load_one(
        near, filters_hbm.at[:, :, wanted], taken_filters_hbm.at[:, :, wanted], filters_ref, sem
    )
    norms = jnp.where(near, norms_ref[...], taken_norms_ref[...])
    odd_sign = jnp.where(space == 0, 1.0, -1.0)
    forward = [tables_ref[part, 0, : 2 * kept, :width] for part in range(2)]
    backward = [tables_ref[part, 1, :width, : 2 * kept] for part in range(2)]
    load.wait()
    for row in range(rows):
        centred, factor = centre(state_ref[row].astype(jnp.float32))
        grid_ref[rows + row] = row_spectra(half == 0, centred, factor, norms, forward)
    mixing_ref[...] = jnp.zeros_like(mixing_ref)
    own_load.wait()
    first, second = pl.ds(0, side), pl.ds(GROUP_LANES, side)
    for layer in range(2):
        for group in range(groups):
            real = filters_ref[layer, 0, group].astype(jnp.bfloat16)
            imag = filters_ref[layer, 1, group].astype(jnp.bfloat16)
            mixing_ref[layer, group, first, first] = real
            mixing_ref[layer, group, first, second] = imag
            mixing_ref[layer, group, second, first] = -imag
            mixing_ref[layer, group, second, second] = real

    def turn(step, carry):
        low = pl.multiple_of(step * 8, 8)
        for group in range(groups):
            lanes = pl.ds(GROUP_LANES * group, GROUP_LANES)
            values = []
            for h in range(12):
                source = near_grid_ref if h < rows else grid_ref
                values.append(
                    (source[h, pl.ds(low, 8), lanes], source[h, pl.ds(kept + low, 8), lanes])
                )
            for k, (real, imag) in enumerate(twelve_point(values, -1)):
                at = pl.ds(k * kept + low, 8)
                if k % 2 == 1:
                    real, imag = real * odd_sign, imag * odd_sign
                modes_ref[group, at, pl.ds(0, GROUP_LANES)] = real
                modes_ref[group, at, pl.ds(GROUP_LANES, GROUP_LANES)] = imag
        return carry

    lax.fori_loop(0, kept // 8, turn, 0)
    for group in range(groups):
        u = jax.nn.relu(dot(modes_ref[group].astype(jnp.bfloat16), mixing_ref[0, group]))
        v = dot(u.astype(jnp.bfloat16), mixing_ref[1, group])
        modes_ref[group] = v - jnp.clip(v, -SHRINK_LEVEL, SHRINK_LEVEL)

    def turn_back(step, carry):
        low = pl.multiple_of(step * 8, 8)
        for group in range(groups):
            lanes = pl.ds(GROUP_LANES * group, GROUP_LANES)
            values = []
            for k in range(12):
                at = pl.ds(k * kept + low, 8)
                real = modes_ref[group, at, pl.ds(0, GROUP_LANES)]
                imag = modes_ref[group, at, pl.ds(GROUP_LANES, GROUP_LANES)]
                if k % 2 == 1:
                    real, imag = real * odd_sign, imag * odd_sign
                values.append((real, imag))
            for h, (real, imag) in enumerate(twelve_point(values, 1)):
                grid_ref[h, pl.ds(low, 8), lanes] = real
                grid_ref[h, pl.ds(kept + low, 8), lanes] = imag
        return carry

    lax.fori_loop(0, kept // 8, turn_back, 0)
    for row in range(2 * rows):
        spectra = grid_ref[row].astype(jnp.bfloat16)
        filtered = dot(backward[0], spectra) + dot(backward[1], spectra)
        out_ref[row] = gather_groups(filtered).astype(out_ref.dtype)


def start_loads(near, near_refs, far_refs, targets, sems):
    def copies(refs):
        return [
            pltpu.make_async_copy(ref, target, sems.at[number])
            for number, (ref, target) in enumerate(zip(refs, targets))
        ]

    @pl.when(near)
    def _():
        for copy in copies(near_refs):
            copy.start()

    @pl.when(jnp.logical_not(near))
    def _():
        for copy in copies(far_refs):
            copy.start()

    return copies(near_refs)


def hidden_kernel(
    count,
    scalars_ref,
    near_base_ref,
    far_base_ref,
    mine_ref,
    theirs_ref,
    norms_ref,
    taken_norms_ref,
    held_ref,
    first_ref,
    second_ref,
    third_ref,
    relayed_ref,
    down_held_ref,
    down_first_ref,
    partial_ref,
    hidden_ref,
    rows_ref,
    up_ref,
    down_ref,
    sems,
    down_sem,
):
    half, space, member = scalars_ref[0], scalars_ref[1], scalars_ref[2]
    near = half == space
    rows, width, channels = near_base_ref.shape
    down_load = load_one(near, down_held_ref, down_first_ref, down_ref, down_sem)
    depth = held_ref.shape[0]
    here, away = 2 * space, 2 * (1 - space)
    order = [here + member, here + 1 - member, away + member, away + 1 - member]
    loads = start_loads(
        near,
        [held_ref, first_ref, second_ref, relayed_ref],
        [second_ref, third_ref, first_ref, relayed_ref],
        [up_ref.at[pl.ds(pl.multiple_of(shard * depth, depth), depth)] for shard in order],
        sems,
    )
    rows_ref[...] = jnp.zeros_like(rows_ref)
    norms = jnp.where(near, norms_ref[...], taken_norms_ref[...])

    def enter_row(part, row):
        mine = mine_ref[part * rows + row].astype(jnp.float32)
        theirs = theirs_ref[part * rows + row].astype(jnp.float32)
        low = jnp.where(half == 0, mine, theirs)
        high = jnp.where(half == 0, theirs, mine)
        base = (near_base_ref, far_base_ref)[part][row]
        blended = base + jnp.concatenate([low, high], 1)
        centred, factor = centre(blended)
        again = centred * factor * norms[1:2] + norms[3:4]
        place = row // count * 2 * count + part * count + row % count
        rows_ref[pl.ds(ROW_STEP * place, width)] = again.astype(jnp.bfloat16)
        own = near if part == 0 else jnp.logical_not(near)
        partial_ref[part * rows + row] = jnp.where(own, blended, 0.0)

    step = up_ref.shape[1] // 2
    columns = [pl.ds(pl.multiple_of(m * step, step), step) for m in (member, 1 - member)]
    for block in range(rows // count):
        for row in range(count * block, count * block + count):
            enter_row(0, row)
            enter_row(1, row)
        if block == 0:
            for copy in loads:
                copy.wait()
            down_load.wait()
        at = pl.ds(2 * count * ROW_STEP * block, 2 * count * ROW_STEP)
        values = rows_ref[at]
        hidden = gelu(dot(values, up_ref[:, columns[0]])).astype(jnp.bfloat16)
        update = dot(hidden, down_ref[...])
        for part in range(2):
            for row in range(count):
                start = ROW_STEP * (part * count + row)
                partial_ref[part * rows + count * block + row] += update[start : start + width]
        hidden_ref[at] = gelu(dot(values, up_ref[:, columns[1]])).astype(jnp.bfloat16)


def update_kernel(
    number,
    scalars_ref,
    partial_ref,
    hidden_ref,
    first_ref,
    second_ref,
    own_ref,
    other_ref,
    down_ref,
    sem,
):
    near = scalars_ref[0] == scalars_ref[1]
    load = load_one(near, first_ref, second_ref, down_ref, sem)
    count, width, _ = own_ref.shape
    rows = partial_ref.shape[0] // 2
    size = count * ROW_STEP
    own_part = jnp.where(near, 0, 1)
    load.wait()
    for target, part in ((other_ref, 1 - own_part), (own_ref, own_part)):
        here = pl.ds(pl.multiple_of(2 * size * number + part * size, size), size)
        update = dot(hidden_ref[here], down_ref[...])
        for row in range(count):
            more = update[ROW_STEP * row : ROW_STEP * row + width]
            value = partial_ref[part * rows + count * number + row] + more
            target[row] = value.astype(target.dtype)


def place_kernel(start, chunk_ref, out_ref, sem):
    copy = pltpu.make_async_copy(chunk_ref, out_ref.at[pl.ds(start, chunk_ref.shape[0])], sem)
    copy.start()
    copy.wait()


def collect_kernel(relayed_ref, *refs):
    sources, out_ref, sems = refs[:-3], refs[-2], refs[-1]
    parts = len(sources) // 2
    count = sources[0].shape[0]

    def copies(step):
        return [
            pltpu.make_async_copy(
                sources[2 * part + step],
                out_ref.at[pl.ds(count * part, count)],
                sems.at[part],
            )
            for part in range(parts)
        ]

    for step in range(2):

        @pl.when(relayed_ref[0] == step)
        def _():
            for copy in copies(step):
                copy.start()

    for copy in copies(0):
        copy.wait()


VMEM = pltpu.VMEM
SCALARS = pl.BlockSpec(memory_space=pltpu.SMEM)
WHOLE = pl.BlockSpec(memory_space=pltpu.VMEM)
LEFT = pl.BlockSpec(memory_space=pltpu.HBM)


def cost(microseconds):
    return pl.CostEstimate(
        flops=int(microseconds * 2e8), bytes_accessed=0, transcendentals=0
    )


def params(megabytes):
    return pltpu.CompilerParams(vmem_limit_bytes=megabytes * 2**20)


def fast_on_device(
    sizes,
    state_in,
    member_ids,
    member_table,
    pos_embed,
    readout_tile_matrix,
    tile_lifting_matrix,
    norm_gain,
    norm_shift,
    spectral,
    up_weight,
    down_weight,
):
    segments, spaces, members = sizes
    position = lax.axis_index("segment")
    core = position % 2
    space = lax.axis_index("space")
    member = lax.axis_index("ens")
    near = core == space

    def table(target):
        pairs = []
        for g in range(segments):
            for s in range(spaces):
                for e in range(members):
                    to = target(g, s, e)
                    if to is not None:
                        flat = (to[0] * spaces + to[1]) * members + to[2]
                        pairs.append(((g * spaces + s) * members + e, flat))
        return pairs

    def send(value, pairs):
        return lax.ppermute(value, MESH_AXES, pairs)

    def keeps(g, s):
        return g % 2 == s

    def moved_place(g, s, e):
        return (g // 2 * 2 + s, g % 2, e)

    far_relocate = table(lambda g, s, e: None if keeps(g, s) else moved_place(g, s, e))
    first_way = table(lambda g, s, e: (g, s, 1 - e) if keeps(g, s) else moved_place(g, s, e))
    second_way = table(lambda g, s, e: (g ^ 1, s, e) if keeps(g, s) else (g, 1 - s, e))
    far_diagonal = table(
        lambda g, s, e: None if keeps(g, s) else moved_place(g, s, 1 - e)
    )
    across = table(lambda g, s, e: (g, s, 1 - e))
    third_way = table(lambda g, s, e: (g ^ 1, s, 1 - e) if keeps(g, s) else None)
    far_to_other = table(lambda g, s, e: (g ^ 1, s, e) if not keeps(g, s) else None)
    swap_cores = table(lambda g, s, e: (g ^ 1, s, e))
    near_to_other = table(lambda g, s, e: (g ^ 1, s, e) if keeps(g, s) else None)
    onward = table(lambda g, s, e: ((g // 2 * 2 + s + 1) % segments, g % 2, e))
    onward_by_space = table(
        lambda g, s, e: (g, 0, e)
        if s == 1 and g % 2 == 0
        else ((g // 2 * 2 + s + 1) % segments, g % 2, e)
    )
    onward_rest = table(
        lambda g, s, e: ((g + 2) % segments, 0, e) if s == 0 and g % 2 == 0 else None
    )

    state = state_in[0, 0, 0]
    rows, width, channels = state.shape
    latitudes = rows * spaces
    bf16, f32, i32 = jnp.bfloat16, jnp.float32, jnp.int32
    up, down = up_weight[0], down_weight[0]
    hidden_half = up.shape[1] // 2

    up_held = lax.dynamic_slice_in_dim(up, space * hidden_half, hidden_half, 1)
    up_held, up_again = lax.optimization_barrier((up_held, up))
    up_given = lax.dynamic_slice_in_dim(up_again, (1 - space) * hidden_half, hidden_half, 1)
    up_first = send(up_held, first_way)
    up_second = send(up_given, second_way)
    entered = pl.pallas_call(
        enter_kernel,
        out_shape=VMEM(state.shape, bf16),
        in_specs=[SCALARS, WHOLE] + [LEFT] * 4,
        out_specs=WHOLE,
        scratch_shapes=[
            VMEM(readout_tile_matrix.shape, bf16),
            VMEM(tile_lifting_matrix.shape, bf16),
            VMEM(pos_embed.shape, bf16),
            VMEM(member_table.shape, bf16),
            VMEM((rows * ROW_STEP, channels), bf16),
            pltpu.SemaphoreType.DMA((4,)),
        ],
        cost_estimate=cost(9),
        compiler_params=params(58),
    )(
        jnp.stack([position, member_ids[0, 0, 0]]).astype(i32),
        state,
        readout_tile_matrix,
        tile_lifting_matrix,
        pos_embed,
        member_table,
    )
    up_third = send(up_given, third_way)
    entered, up_first, up_second, up_third = lax.optimization_barrier(
        (entered, up_first, up_second, up_third)
    )
    moved = send(entered, far_relocate)
    near_state = send(entered, near_to_other)
    up_relayed = send(jnp.where(near, up_second, up_first), across)
    norms = jnp.concatenate([norm_gain[0], norm_shift[0]], 0)
    taken_norms = send(norms, near_to_other)
    filters = spectral[0]
    taken_filters = send(filters, near_to_other)
    scalars = jnp.stack([core, space, member]).astype(i32)
    tables = jnp.asarray(split_longitude_tables(width, KW, latitudes))
    half_groups = spectral.shape[3] // 2
    lanes = half_groups * GROUP_LANES
    near_grid, near_base = pl.pallas_call(
        near_kernel,
        out_shape=[VMEM((rows, 2 * KW, lanes), f32), VMEM(state.shape, f32)],
        in_specs=[SCALARS] + [LEFT] * 2 + [WHOLE] * 3,
        out_specs=[WHOLE] * 2,
        scratch_shapes=[VMEM(state.shape, bf16), pltpu.SemaphoreType.DMA],
        cost_estimate=cost(5),
        compiler_params=params(12),
    )(scalars, entered, near_state, norms, taken_norms, tables)
    moved, near_grid, up_relayed, taken_filters, down_later = lax.optimization_barrier(
        (moved, near_grid, up_relayed, taken_filters, down)
    )
    far_state = send(moved, far_to_other)
    down_first = send(down_later, first_way)
    filtered = pl.pallas_call(
        filter_kernel,
        out_shape=jax.ShapeDtypeStruct((2 * rows, width, channels // 2), bf16),
        in_specs=[SCALARS] + [LEFT] * 2 + [WHOLE] * 4 + [LEFT] * 2,
        out_specs=WHOLE,
        scratch_shapes=[
            VMEM((latitudes, 2 * KW, lanes), f32),
            VMEM((half_groups, latitudes * KW, 2 * GROUP_LANES), f32),
            VMEM((2, 2, half_groups) + filters.shape[3:], f32),
            VMEM((2, half_groups, 2 * GROUP_LANES, 2 * GROUP_LANES), bf16),
            VMEM(state.shape, bf16),
            pltpu.SemaphoreType.DMA,
            pltpu.SemaphoreType.DMA,
        ],
        cost_estimate=cost(11),
        compiler_params=params(24),
    )(
        scalars,
        moved,
        far_state,
        norms,
        taken_norms,
        tables,
        near_grid,
        filters,
        taken_filters,
    )
    filtered, down_first, up_relayed, down_again = lax.optimization_barrier(
        (filtered, down_first, up_relayed, down)
    )
    down_second = send(down_again, far_diagonal)
    filtered_other = send(filtered, swap_cores)
    scalars_later, _ = lax.optimization_barrier((scalars, filtered))
    far_base = pl.pallas_call(
        base_kernel,
        out_shape=VMEM(state.shape, f32),
        in_specs=[SCALARS] + [LEFT] * 2 + [WHOLE] * 2,
        out_specs=WHOLE,
        scratch_shapes=[VMEM(state.shape, bf16), pltpu.SemaphoreType.DMA],
        cost_estimate=cost(3),
        compiler_params=params(12),
    )(scalars_later, moved, far_state, norms, taken_norms)

    parts = 2
    partial, hidden = pl.pallas_call(
        functools.partial(hidden_kernel, rows // parts),
        out_shape=[
            VMEM((2 * rows, width, channels), f32),
            VMEM((2 * rows * ROW_STEP, hidden_half // 2), bf16),
        ],
        in_specs=[SCALARS] + [WHOLE] * 6 + [LEFT] * 7,
        out_specs=[WHOLE] * 2,
        scratch_shapes=[
            VMEM((2 * rows * ROW_STEP, channels), bf16),
            VMEM((channels, hidden_half), bf16),
            VMEM((hidden_half // 2, channels), bf16),
            pltpu.SemaphoreType.DMA((4,)),
            pltpu.SemaphoreType.DMA,
        ],
        cost_estimate=cost(11),
        compiler_params=params(26),
    )(
        scalars,
        near_base,
        far_base,
        filtered,
        filtered_other,
        norms,
        taken_norms,
        up_held,
        up_first,
        up_second,
        up_third,
        up_relayed,
        down,
        down_first,
    )
    landed, ready = [], []
    for number in range(parts):
        own, other = pl.pallas_call(
            functools.partial(update_kernel, number),
            out_shape=[
                jax.ShapeDtypeStruct((rows // parts, width, channels), f32),
                jax.ShapeDtypeStruct((rows // parts, width, channels), bf16),
            ],
            in_specs=[SCALARS] + [WHOLE] * 2 + [LEFT] * 2,
            out_specs=[WHOLE] * 2,
            scratch_shapes=[
                VMEM((hidden_half // 2, channels), bf16),
                pltpu.SemaphoreType.DMA,
            ],
            cost_estimate=cost(50),
            compiler_params=params(24),
        )(scalars, partial, hidden, down_first, down_second)
        ready.append((own + send(other, swap_cores).astype(f32)).astype(bf16))
        if number + 1 < parts:
            landed.append([send(ready[-1], onward_by_space)])
        else:
            landed.append([send(ready[-1], onward)])
    for number in range(parts - 1):
        first_hop = landed[number][0]
        if number > 0:
            first_hop, _ = lax.optimization_barrier((first_hop, ready[-1]))
        landed[number].append(send(first_hop, onward_rest))
    relayed = (core + space == 0).astype(i32)[None]
    out = pl.pallas_call(
        functools.partial(place_kernel, rows // parts * (parts - 1)),
        out_shape=jax.ShapeDtypeStruct(state.shape, bf16),
        in_specs=[WHOLE],
        out_specs=LEFT,
        scratch_shapes=[pltpu.SemaphoreType.DMA],
        cost_estimate=cost(100),
        compiler_params=params(16),
    )(landed[-1][0])
    arrived = [value for chunk in landed[:-1] for value in chunk]
    out = pl.pallas_call(
        collect_kernel,
        out_shape=jax.ShapeDtypeStruct(state.shape, bf16),
        in_specs=[SCALARS] + [WHOLE] * len(arrived) + [LEFT],
        out_specs=LEFT,
        input_output_aliases={1 + len(arrived): 0},
        scratch_shapes=[pltpu.SemaphoreType.DMA((parts - 1,))],
        compiler_params=params(16),
    )(relayed, *arrived, out)
    return out[None, None, None]


def solution(mesh):
    placed = (
        P("ens", "segment", None, "space", None, None),
        P("ens", None, None),
        P(),
        P("space", None, None),
        P(),
        P(),
        P("segment", None, None),
        P("segment", None, None),
        P("segment", None, None, None, None, None),
        P("segment", ("space", "ens"), None),
        P("segment", ("space", "ens"), None),
    )
    sizes = tuple(mesh.shape[axis] for axis in MESH_AXES)
    whole_micro_batch_on_a_chip = sizes[0] % 2 == 0 and sizes[1:] == (2, 2)
    if whole_micro_batch_on_a_chip:
        program = functools.partial(fast_on_device, sizes)
    else:
        program = on_device
    return jax.shard_map(
        program,
        mesh=mesh,
        in_specs=placed,
        out_specs=P("ens", "segment", None, "space", None, None),
        check_vma=False,
    )
```

```python
import functools
import math

import jax
import jax.numpy as jnp
import ml_dtypes
import numpy as np
from jax import lax
from jax.experimental import pallas as pl
from jax.experimental.pallas import tpu as pltpu
from jax.sharding import PartitionSpec as P

KW = 88


EPSILON = 1e-05
SHRINK_LEVEL = 0.01
HIGHEST_PRECISION = lax.Precision.HIGHEST


def shifted(value, axis, steps):
    count = lax.axis_size(axis)
    pairs = [(source, (source + steps) % count) for source in range(count)]
    return lax.ppermute(value, axis, pairs)


def layer_norm(values):
    average = jnp.mean(values, axis=-1, keepdims=True)
    centred = values - average
    spread = jnp.mean(centred * centred, axis=-1, keepdims=True)
    return centred * lax.rsqrt(spread + EPSILON)


def longitude_tables(longitudes, kept, latitudes):
    number = jnp.arange(kept, dtype=jnp.int32)[:, None]
    points = jnp.arange(longitudes, dtype=jnp.int32)[None, :]
    angles = (number * points % longitudes).astype(jnp.float32) * (2.0 * math.pi / longitudes)
    factor = 1.0 / math.sqrt(latitudes * longitudes)
    doubled = jnp.where(number == 0, 1.0, 2.0).astype(jnp.float32) * factor
    forward = jnp.stack([jnp.cos(angles) * factor, -jnp.sin(angles) * factor])
    backward = jnp.stack([jnp.cos(angles) * doubled, -jnp.sin(angles) * doubled])
    return (forward, backward)


def latitude_tables(latitudes):
    number = jnp.arange(latitudes, dtype=jnp.int32)[:, None]
    points = jnp.arange(latitudes, dtype=jnp.int32)[None, :]
    angles = (number * points % latitudes).astype(jnp.float32) * (2.0 * math.pi / latitudes)
    cosine_table = jnp.cos(angles)
    sine_table = jnp.sin(angles)
    forward = jnp.concatenate(
        [
            jnp.concatenate([cosine_table, sine_table], 1),
            jnp.concatenate([-sine_table, cosine_table], 1),
        ],
        0,
    )
    backward = jnp.concatenate(
        [
            jnp.concatenate([cosine_table, -sine_table], 1),
            jnp.concatenate([sine_table, cosine_table], 1),
        ],
        0,
    )
    return (forward, backward)


def mix_blocks(spectra, filters):
    extent = spectra.shape
    halves = spectra.reshape(extent[0], 2, extent[2], extent[3], filters.shape[2], filters.shape[3])
    nonimaginary_component = halves[:, 0]
    imag_part = halves[:, 1]

    def product(operand, matrix):
        return jnp.einsum("mhknb,nbc->mhknc", operand, matrix, precision=HIGHEST_PRECISION)

    first_real = jax.nn.relu(
        product(nonimaginary_component, filters[0, 0]) - product(imag_part, filters[0, 1])
    )
    first_imag = jax.nn.relu(
        product(nonimaginary_component, filters[0, 1]) + product(imag_part, filters[0, 0])
    )
    second_real = product(first_real, filters[1, 0]) - product(first_imag, filters[1, 1])
    second_imag = product(first_real, filters[1, 1]) + product(first_imag, filters[1, 0])
    blended = jnp.stack([second_real, second_imag], axis=1)
    blended = blended - jnp.clip(blended, -SHRINK_LEVEL, SHRINK_LEVEL)
    return blended.reshape(extent)


def spectral_filter(normed_one, filters, tables):
    forward, backward, lat_forward, lat_backward = tables
    spectra = jnp.einsum("rkw,mhwd->mrhkd", forward, normed_one, precision=HIGHEST_PRECISION)
    collected_fields = lax.all_to_all(spectra, "space", split_axis=3, concat_axis=2, tiled=True)
    extent = collected_fields.shape
    stacked = collected_fields.reshape(extent[0], 2 * extent[2], extent[3], extent[4])
    turned = jnp.einsum("ab,mbkd->makd", lat_forward, stacked, precision=HIGHEST_PRECISION)
    blended_modes = mix_blocks(turned.reshape(extent), filters).reshape(stacked.shape)
    inverse = jnp.einsum(
        "ab,mbkd->makd", lat_backward, blended_modes, precision=HIGHEST_PRECISION
    ).reshape(extent)
    returned = lax.all_to_all(inverse, "space", split_axis=2, concat_axis=3, tiled=True)
    return jnp.einsum("rkw,mrhkd->mhwd", backward, returned, precision=HIGHEST_PRECISION)


def on_device(
    state_in,
    member_ids,
    member_table,
    pos_embed,
    readout_tile_matrix,
    tile_lifting_matrix,
    norm_gain,
    norm_shift,
    spectral,
    up_weight,
    down_weight,
):
    position = lax.axis_index("segment")
    segment_count = lax.axis_size("segment")
    current = state_in[0, 0]
    channels = current.shape[3]
    latitudes = current.shape[1] * lax.axis_size("space")
    forward, backward = longitude_tables(current.shape[2], KW, latitudes)
    lat_forward, lat_backward = latitude_tables(latitudes)
    tables = (forward, backward, lat_forward, lat_backward)
    gains = norm_gain[0]
    shifts = norm_shift[0]
    filters = spectral[0]
    slot_index = -0 % segment_count
    chosen = member_ids[0, slot_index]
    onehot = (
        chosen[:, None] == jnp.arange(member_table.shape[0], dtype=jnp.int32)[None, :]
    ).astype(jnp.bfloat16)
    sample_trajectory_lines = jnp.dot(onehot, member_table, preferred_element_type=jnp.float32)

    def enter_grid(values):
        standardized_field = layer_norm(values.astype(jnp.float32)).astype(jnp.bfloat16)
        prediction_increment = jnp.einsum(
            "fbrd,do->fbro",
            standardized_field,
            readout_tile_matrix,
            preferred_element_type=jnp.float32,
        ).astype(jnp.bfloat16)
        admitted_lines = jnp.einsum(
            "nzwt,tl->nzwl",
            prediction_increment,
            tile_lifting_matrix,
            preferred_element_type=jnp.float32,
        )
        return (
            admitted_lines
            + pos_embed.astype(jnp.float32)[None]
            + sample_trajectory_lines[:, None, None, :]
        )

    def cast_values(values):
        return values.astype(jnp.float32)

    carried = lax.cond(position == 0, enter_grid, cast_values, current)
    normed_one = layer_norm(carried) * gains[0] + shifts[0]
    blended = carried + normed_one + spectral_filter(normed_one, filters, tables)
    normed_two = (layer_norm(blended) * gains[1] + shifts[1]).astype(jnp.bfloat16)
    flat_rows = normed_two.reshape(-1, channels)
    columns = flat_rows
    lifted = jnp.dot(
        columns,
        lax.all_gather(up_weight, ("space", "ens"), axis=1, tiled=True)[0],
        preferred_element_type=jnp.float32,
    )
    hidden = jax.nn.gelu(lifted, approximate=False).astype(jnp.bfloat16)
    columns = hidden
    update = jnp.dot(
        columns,
        lax.all_gather(down_weight, ("space", "ens"), axis=1, tiled=True)[0],
        preferred_element_type=jnp.float32,
    ).reshape(blended.shape)
    current = shifted((blended + update).astype(jnp.bfloat16), "segment", 1)
    return current[None, None]


ROW_STEP = 192
GROUP_LANES = 128
MESH_AXES = ("segment", "space", "ens")


def split_table(table):
    high = table.astype(ml_dtypes.bfloat16)
    low = (table - high.astype(np.float64)).astype(ml_dtypes.bfloat16)
    return np.stack([high, low])


def split_longitude_tables(longitudes, kept, latitudes):
    number = np.arange(kept)[:, None]
    points = np.arange(longitudes)[None, :]
    angles = (number * points % longitudes) * (2.0 * math.pi / longitudes)
    factor = 1.0 / math.sqrt(latitudes * longitudes)
    doubled = np.where(number == 0, 1.0, 2.0) * factor
    forward = np.concatenate([np.cos(angles) * factor, -np.sin(angles) * factor], 0)
    backward = np.concatenate([np.cos(angles) * doubled, -np.sin(angles) * doubled], 0).T
    size = max(forward.shape)
    both = np.zeros((2, size, size))
    both[0, : forward.shape[0], : forward.shape[1]] = forward
    both[1, : backward.shape[0], : backward.shape[1]] = backward
    return split_table(both)


def three_point(x, sign):
    (ar, ai), (br, bi), (cr, ci) = x
    tr, ti = br + cr, bi + ci
    mr, mi = ar - 0.5 * tr, ai - 0.5 * ti
    scale = math.sin(math.pi / 3.0) * sign
    dr, di = (br - cr) * scale, (bi - ci) * scale
    return [(ar + tr, ai + ti), (mr - di, mi + dr), (mr + di, mi - dr)]


def four_point(x, sign):
    (ar, ai), (br, bi), (cr, ci), (dr, di) = x
    sr, si, tr, ti = ar + cr, ai + ci, ar - cr, ai - ci
    ur, ui, vr, vi = br + dr, bi + di, br - dr, bi - di
    plus, minus = (tr - vi, ti + vr), (tr + vi, ti - vr)
    if sign < 0:
        plus, minus = minus, plus
    return [(sr + ur, si + ui), plus, (sr - ur, si - ui), minus]


def twelve_point(x, sign):
    columns = [three_point([x[(4 * a + 3 * b) % 12] for a in range(3)], sign) for b in range(4)]
    out = [None] * 12
    for a in range(3):
        line = four_point([columns[b][a] for b in range(4)], sign)
        for b in range(4):
            out[(4 * a + 9 * b) % 12] = line[b]
    return out


def lane_index(shape):
    return lax.broadcasted_iota(jnp.int32, shape, len(shape) - 1)


def spread_groups(values):
    a, b, c = (values[:, 128 * i : 128 * i + 128] for i in range(3))
    lanes = lane_index(a.shape)
    second = jnp.where(lanes < 32, pltpu.roll(a, 32, 1), pltpu.roll(b, 32, 1))
    third = jnp.where(lanes < 64, pltpu.roll(b, 64, 1), pltpu.roll(c, 64, 1))
    return jnp.concatenate([a, second, third, pltpu.roll(c, 96, 1)], 1)


def gather_groups(values):
    a, b, c, d = (values[:, 128 * i : 128 * i + 128] for i in range(4))
    lanes = lane_index(a.shape)
    first = jnp.where(lanes < 96, a, pltpu.roll(b, 96, 1))
    second = jnp.where(lanes < 64, pltpu.roll(b, 96, 1), pltpu.roll(c, 64, 1))
    third = jnp.where(lanes < 32, pltpu.roll(c, 64, 1), pltpu.roll(d, 32, 1))
    return jnp.concatenate([first, second, third], 1)


def gelu(x):
    return 0.5 * x * (1.0 + lax.erf(x * math.sqrt(0.5)))


def enter_kernel(
    scalars_ref,
    state_ref,
    readout_hbm,
    lifting_hbm,
    pos_hbm,
    table_hbm,
    out_ref,
    readout_ref,
    lifting_ref,
    pos_ref,
    table_ref,
    rows_ref,
    sems,
):
    first_segment, member = scalars_ref[0] == 0, scalars_ref[1]
    rows, width = state_ref.shape[:2]

    @pl.when(first_segment)
    def _():
        pairs = (
            (readout_hbm, readout_ref),
            (lifting_hbm, lifting_ref),
            (pos_hbm, pos_ref),
            (table_hbm, table_ref),
        )
        loads = [
            pltpu.make_async_copy(source, target, sems.at[number])
            for number, (source, target) in enumerate(pairs)
        ]
        for load in loads:
            load.start()
        rows_ref[...] = jnp.zeros_like(rows_ref)
        for row in range(rows):
            normed = layer_norm(state_ref[row].astype(jnp.float32)).astype(jnp.bfloat16)
            rows_ref[pl.ds(ROW_STEP * row, width)] = normed
        loads[0].wait()
        loads[3].wait()
        members = table_ref.shape[0]
        chosen = lax.broadcasted_iota(jnp.int32, (8, members), 1) == member
        line = jnp.dot(
            jnp.where(chosen, 1.0, 0.0).astype(jnp.bfloat16),
            table_ref[...],
            preferred_element_type=jnp.float32,
        )[0:1]
        for first in range(0, rows, 2):
            block = rows_ref[pl.ds(ROW_STEP * first, 2 * ROW_STEP)]
            forecast = jnp.dot(block, readout_ref[...], preferred_element_type=jnp.float32)
            if first == 0:
                loads[1].wait()
                loads[2].wait()
            lifted = jnp.dot(
                forecast.astype(jnp.bfloat16), lifting_ref[...], preferred_element_type=jnp.float32
            )
            for row in range(2):
                part = lifted[ROW_STEP * row : ROW_STEP * row + width]
                carried = part + pos_ref[first + row].astype(jnp.float32) + line
                out_ref[first + row] = carried.astype(jnp.bfloat16)

    @pl.when(jnp.logical_not(first_segment))
    def _():
        out_ref[...] = state_ref[...]


def load_one(near, near_ref, far_ref, target, sem):
    near_copy = pltpu.make_async_copy(near_ref, target, sem)
    far_copy = pltpu.make_async_copy(far_ref, target, sem)
    pl.when(near)(near_copy.start)
    pl.when(jnp.logical_not(near))(far_copy.start)
    return near_copy


def centre(values):
    average = jnp.mean(values, axis=-1, keepdims=True)
    centred = values - average
    spread = jnp.mean(centred * centred, axis=-1, keepdims=True)
    return centred, lax.rsqrt(spread + EPSILON)


def dot(a, b):
    return jnp.dot(a, b, preferred_element_type=jnp.float32)


def row_spectra(lower, centred, factor, norms, forward):
    channels = centred.shape[1] // 2

    def chosen(values):
        return jnp.where(lower, values[:, :channels], values[:, channels:])

    normed = chosen(centred) * factor * chosen(norms[0:1]) + chosen(norms[2:3])
    points = spread_groups(normed).astype(jnp.bfloat16)
    return dot(forward[0], points) + dot(forward[1], points)


def near_kernel(
    scalars_ref,
    entered_ref,
    near_state_ref,
    norms_ref,
    taken_norms_ref,
    tables_ref,
    grid_ref,
    base_ref,
    state_ref,
    sem,
):
    half, space = scalars_ref[0], scalars_ref[1]
    near = half == space
    load = load_one(near, entered_ref, near_state_ref, state_ref, sem)
    rows, width, _ = state_ref.shape
    norms = jnp.where(near, norms_ref[...], taken_norms_ref[...])
    forward = [tables_ref[part, 0, : grid_ref.shape[1], :width] for part in range(2)]
    load.wait()
    for row in range(rows):
        carried = state_ref[row].astype(jnp.float32)
        centred, factor = centre(carried)
        base_ref[row] = carried + (centred * factor * norms[0:1] + norms[2:3])
        grid_ref[row] = row_spectra(half == 0, centred, factor, norms, forward)


def filter_kernel(
    scalars_ref,
    moved_ref,
    far_state_ref,
    norms_ref,
    taken_norms_ref,
    tables_ref,
    near_grid_ref,
    filters_hbm,
    taken_filters_hbm,
    out_ref,
    base_ref,
    grid_ref,
    modes_ref,
    filters_ref,
    mixing_ref,
    state_ref,
    sem,
    state_sem,
):
    half, space = scalars_ref[0], scalars_ref[1]
    near = half == space
    load = load_one(near, far_state_ref, moved_ref, state_ref, state_sem)
    rows, width, _ = state_ref.shape
    kept = grid_ref.shape[1] // 2
    groups = modes_ref.shape[0]
    side = filters_ref.shape[-1]
    wanted = pl.ds(half * groups, groups)
    own_load = load_one(
        near, filters_hbm.at[:, :, wanted], taken_filters_hbm.at[:, :, wanted], filters_ref, sem
    )
    norms = jnp.where(near, norms_ref[...], taken_norms_ref[...])
    odd_sign = jnp.where(space == 0, 1.0, -1.0)
    forward = [tables_ref[part, 0, : 2 * kept, :width] for part in range(2)]
    backward = [tables_ref[part, 1, :width, : 2 * kept] for part in range(2)]
    load.wait()
    for row in range(rows):
        carried = state_ref[row].astype(jnp.float32)
        centred, factor = centre(carried)
        base_ref[row] = carried + (centred * factor * norms[0:1] + norms[2:3])
        grid_ref[rows + row] = row_spectra(half == 0, centred, factor, norms, forward)
    mixing_ref[...] = jnp.zeros_like(mixing_ref)
    own_load.wait()
    first, second = pl.ds(0, side), pl.ds(GROUP_LANES, side)
    for layer in range(2):
        for group in range(groups):
            real = filters_ref[layer, 0, group].astype(jnp.bfloat16)
            imag = filters_ref[layer, 1, group].astype(jnp.bfloat16)
            mixing_ref[layer, group, first, first] = real
            mixing_ref[layer, group, first, second] = imag
            mixing_ref[layer, group, second, first] = -imag
            mixing_ref[layer, group, second, second] = real

    def turn(step, carry):
        low = pl.multiple_of(step * 8, 8)
        for group in range(groups):
            lanes = pl.ds(GROUP_LANES * group, GROUP_LANES)
            values = []
            for h in range(12):
                source = near_grid_ref if h < rows else grid_ref
                values.append(
                    (source[h, pl.ds(low, 8), lanes], source[h, pl.ds(kept + low, 8), lanes])
                )
            for k, (real, imag) in enumerate(twelve_point(values, -1)):
                at = pl.ds(k * kept + low, 8)
                if k % 2 == 1:
                    real, imag = real * odd_sign, imag * odd_sign
                modes_ref[group, at, pl.ds(0, GROUP_LANES)] = real
                modes_ref[group, at, pl.ds(GROUP_LANES, GROUP_LANES)] = imag
        return carry

    lax.fori_loop(0, kept // 8, turn, 0)
    for group in range(groups):
        u = jax.nn.relu(dot(modes_ref[group].astype(jnp.bfloat16), mixing_ref[0, group]))
        v = dot(u.astype(jnp.bfloat16), mixing_ref[1, group])
        modes_ref[group] = v - jnp.clip(v, -SHRINK_LEVEL, SHRINK_LEVEL)

    def turn_back(step, carry):
        low = pl.multiple_of(step * 8, 8)
        for group in range(groups):
            lanes = pl.ds(GROUP_LANES * group, GROUP_LANES)
            values = []
            for k in range(12):
                at = pl.ds(k * kept + low, 8)
                real = modes_ref[group, at, pl.ds(0, GROUP_LANES)]
                imag = modes_ref[group, at, pl.ds(GROUP_LANES, GROUP_LANES)]
                if k % 2 == 1:
                    real, imag = real * odd_sign, imag * odd_sign
                values.append((real, imag))
            for h, (real, imag) in enumerate(twelve_point(values, 1)):
                grid_ref[h, pl.ds(low, 8), lanes] = real
                grid_ref[h, pl.ds(kept + low, 8), lanes] = imag
        return carry

    lax.fori_loop(0, kept // 8, turn_back, 0)
    for row in range(2 * rows):
        spectra = grid_ref[row].astype(jnp.bfloat16)
        filtered = dot(backward[0], spectra) + dot(backward[1], spectra)
        out_ref[row] = gather_groups(filtered).astype(out_ref.dtype)


def start_loads(near, near_refs, far_refs, targets, sems):
    def copies(refs):
        return [
            pltpu.make_async_copy(ref, target, sems.at[number])
            for number, (ref, target) in enumerate(zip(refs, targets))
        ]

    @pl.when(near)
    def _():
        for copy in copies(near_refs):
            copy.start()

    @pl.when(jnp.logical_not(near))
    def _():
        for copy in copies(far_refs):
            copy.start()

    return copies(near_refs)


def hidden_kernel(
    count,
    scalars_ref,
    near_base_ref,
    far_base_ref,
    mine_ref,
    theirs_ref,
    norms_ref,
    taken_norms_ref,
    held_ref,
    first_ref,
    second_ref,
    third_ref,
    relayed_ref,
    down_held_ref,
    down_first_ref,
    partial_ref,
    hidden_ref,
    rows_ref,
    up_ref,
    down_ref,
    sems,
    down_sem,
):
    half, space, member = scalars_ref[0], scalars_ref[1], scalars_ref[2]
    near = half == space
    rows, width, channels = near_base_ref.shape
    down_load = load_one(near, down_held_ref, down_first_ref, down_ref, down_sem)
    depth = held_ref.shape[0]
    here, away = 2 * space, 2 * (1 - space)
    order = [here + member, here + 1 - member, away + member, away + 1 - member]
    loads = start_loads(
        near,
        [held_ref, first_ref, second_ref, relayed_ref],
        [second_ref, third_ref, first_ref, relayed_ref],
        [up_ref.at[pl.ds(pl.multiple_of(shard * depth, depth), depth)] for shard in order],
        sems,
    )
    rows_ref[...] = jnp.zeros_like(rows_ref)
    norms = jnp.where(near, norms_ref[...], taken_norms_ref[...])

    def enter_row(part, row):
        mine = mine_ref[part * rows + row].astype(jnp.float32)
        theirs = theirs_ref[part * rows + row].astype(jnp.float32)
        low = jnp.where(half == 0, mine, theirs)
        high = jnp.where(half == 0, theirs, mine)
        base = (near_base_ref, far_base_ref)[part][row]
        blended = base + jnp.concatenate([low, high], 1)
        centred, factor = centre(blended)
        again = centred * factor * norms[1:2] + norms[3:4]
        place = row // count * 2 * count + part * count + row % count
        rows_ref[pl.ds(ROW_STEP * place, width)] = again.astype(jnp.bfloat16)
        own = near if part == 0 else jnp.logical_not(near)
        partial_ref[part * rows + row] = jnp.where(own, blended, 0.0)

    step = up_ref.shape[1] // 2
    columns = [pl.ds(pl.multiple_of(m * step, step), step) for m in (member, 1 - member)]
    for block in range(rows // count):
        for row in range(count * block, count * block + count):
            enter_row(0, row)
            enter_row(1, row)
        if block == 0:
            for copy in loads:
                copy.wait()
            down_load.wait()
        at = pl.ds(2 * count * ROW_STEP * block, 2 * count * ROW_STEP)
        values = rows_ref[at]
        hidden = gelu(dot(values, up_ref[:, columns[0]])).astype(jnp.bfloat16)
        update = dot(hidden, down_ref[...])
        for part in range(2):
            for row in range(count):
                start = ROW_STEP * (part * count + row)
                partial_ref[part * rows + count * block + row] += update[start : start + width]
        hidden_ref[at] = gelu(dot(values, up_ref[:, columns[1]])).astype(jnp.bfloat16)


def update_kernel(
    number,
    scalars_ref,
    partial_ref,
    hidden_ref,
    first_ref,
    second_ref,
    own_ref,
    other_ref,
    down_ref,
    sem,
):
    near = scalars_ref[0] == scalars_ref[1]
    load = load_one(near, first_ref, second_ref, down_ref, sem)
    count, width, _ = own_ref.shape
    rows = partial_ref.shape[0] // 2
    size = count * ROW_STEP
    own_part = jnp.where(near, 0, 1)
    load.wait()
    for target, part in ((other_ref, 1 - own_part), (own_ref, own_part)):
        here = pl.ds(pl.multiple_of(2 * size * number + part * size, size), size)
        update = dot(hidden_ref[here], down_ref[...])
        for row in range(count):
            more = update[ROW_STEP * row : ROW_STEP * row + width]
            value = partial_ref[part * rows + count * number + row] + more
            target[row] = value.astype(target.dtype)


def place_kernel(start, chunk_ref, out_ref, sem):
    copy = pltpu.make_async_copy(chunk_ref, out_ref.at[pl.ds(start, chunk_ref.shape[0])], sem)
    copy.start()
    copy.wait()


def collect_kernel(relayed_ref, *refs):
    sources, out_ref, sems = refs[:-3], refs[-2], refs[-1]
    parts = len(sources) // 2
    count = sources[0].shape[0]

    def copies(step):
        return [
            pltpu.make_async_copy(
                sources[2 * part + step],
                out_ref.at[pl.ds(count * part, count)],
                sems.at[part],
            )
            for part in range(parts)
        ]

    for step in range(2):

        @pl.when(relayed_ref[0] == step)
        def _():
            for copy in copies(step):
                copy.start()

    for copy in copies(0):
        copy.wait()


VMEM = pltpu.VMEM
SCALARS = pl.BlockSpec(memory_space=pltpu.SMEM)
WHOLE = pl.BlockSpec(memory_space=pltpu.VMEM)
LEFT = pl.BlockSpec(memory_space=pltpu.HBM)


def cost(microseconds):
    return pl.CostEstimate(
        flops=int(microseconds * 2e8), bytes_accessed=0, transcendentals=0
    )


def params(megabytes):
    return pltpu.CompilerParams(vmem_limit_bytes=megabytes * 2**20)


def fast_on_device(
    sizes,
    state_in,
    member_ids,
    member_table,
    pos_embed,
    readout_tile_matrix,
    tile_lifting_matrix,
    norm_gain,
    norm_shift,
    spectral,
    up_weight,
    down_weight,
):
    segments, spaces, members = sizes
    position = lax.axis_index("segment")
    core = position % 2
    space = lax.axis_index("space")
    member = lax.axis_index("ens")
    near = core == space

    def table(target):
        pairs = []
        for g in range(segments):
            for s in range(spaces):
                for e in range(members):
                    to = target(g, s, e)
                    if to is not None:
                        flat = (to[0] * spaces + to[1]) * members + to[2]
                        pairs.append(((g * spaces + s) * members + e, flat))
        return pairs

    def send(value, pairs):
        return lax.ppermute(value, MESH_AXES, pairs)

    def keeps(g, s):
        return g % 2 == s

    def moved_place(g, s, e):
        return (g // 2 * 2 + s, g % 2, e)

    far_relocate = table(lambda g, s, e: None if keeps(g, s) else moved_place(g, s, e))
    first_way = table(lambda g, s, e: (g, s, 1 - e) if keeps(g, s) else moved_place(g, s, e))
    second_way = table(lambda g, s, e: (g ^ 1, s, e) if keeps(g, s) else (g, 1 - s, e))
    far_diagonal = table(
        lambda g, s, e: None if keeps(g, s) else moved_place(g, s, 1 - e)
    )
    across = table(lambda g, s, e: (g, s, 1 - e))
    third_way = table(lambda g, s, e: (g ^ 1, s, 1 - e) if keeps(g, s) else None)
    swap_cores = table(lambda g, s, e: (g ^ 1, s, e))
    onward = table(lambda g, s, e: ((g // 2 * 2 + s + 1) % segments, g % 2, e))
    onward_by_space = table(
        lambda g, s, e: (g, 0, e)
        if s == 1 and g % 2 == 0
        else ((g // 2 * 2 + s + 1) % segments, g % 2, e)
    )
    onward_rest = table(
        lambda g, s, e: ((g + 2) % segments, 0, e) if s == 0 and g % 2 == 0 else None
    )

    state = state_in[0, 0, 0]
    rows, width, channels = state.shape
    latitudes = rows * spaces
    bf16, f32, i32 = jnp.bfloat16, jnp.float32, jnp.int32
    up, down = up_weight[0], down_weight[0]
    hidden_half = up.shape[1] // 2

    up_held = lax.dynamic_slice_in_dim(up, space * hidden_half, hidden_half, 1)
    up_held, up_again = lax.optimization_barrier((up_held, up))
    up_given = lax.dynamic_slice_in_dim(up_again, (1 - space) * hidden_half, hidden_half, 1)
    up_first = send(up_held, first_way)
    up_second = send(up_given, second_way)
    entered = pl.pallas_call(
        enter_kernel,
        out_shape=VMEM(state.shape, bf16),
        in_specs=[SCALARS, WHOLE] + [LEFT] * 4,
        out_specs=WHOLE,
        scratch_shapes=[
            VMEM(readout_tile_matrix.shape, bf16),
            VMEM(tile_lifting_matrix.shape, bf16),
            VMEM(pos_embed.shape, bf16),
            VMEM(member_table.shape, bf16),
            VMEM((rows * ROW_STEP, channels), bf16),
            pltpu.SemaphoreType.DMA((4,)),
        ],
        cost_estimate=cost(9),
        compiler_params=params(58),
    )(
        jnp.stack([position, member_ids[0, 0, 0]]).astype(i32),
        state,
        readout_tile_matrix,
        tile_lifting_matrix,
        pos_embed,
        member_table,
    )
    up_third = send(up_given, third_way)
    entered, up_first, up_second, up_third = lax.optimization_barrier(
        (entered, up_first, up_second, up_third)
    )
    moved = send(entered, far_relocate)
    near_state = send(entered, swap_cores)
    up_relayed = send(jnp.where(near, up_second, up_first), across)
    norms = jnp.concatenate([norm_gain[0], norm_shift[0]], 0)
    taken_norms = send(norms, swap_cores)
    filters = spectral[0]
    taken_filters = send(filters, swap_cores)
    scalars = jnp.stack([core, space, member]).astype(i32)
    tables = jnp.asarray(split_longitude_tables(width, KW, latitudes))
    half_groups = spectral.shape[3] // 2
    lanes = half_groups * GROUP_LANES
    near_grid, near_base = pl.pallas_call(
        near_kernel,
        out_shape=[VMEM((rows, 2 * KW, lanes), f32), VMEM(state.shape, f32)],
        in_specs=[SCALARS] + [LEFT] * 2 + [WHOLE] * 3,
        out_specs=[WHOLE] * 2,
        scratch_shapes=[VMEM(state.shape, bf16), pltpu.SemaphoreType.DMA],
        cost_estimate=cost(5),
        compiler_params=params(12),
    )(scalars, entered, near_state, norms, taken_norms, tables)
    moved, near_grid, up_relayed, taken_filters, down_later = lax.optimization_barrier(
        (moved, near_grid, up_relayed, taken_filters, down)
    )
    far_state = send(moved, swap_cores)
    down_first = send(down_later, first_way)
    filtered, far_base = pl.pallas_call(
        filter_kernel,
        out_shape=[
            jax.ShapeDtypeStruct((2 * rows, width, channels // 2), bf16),
            VMEM(state.shape, f32),
        ],
        in_specs=[SCALARS] + [LEFT] * 2 + [WHOLE] * 4 + [LEFT] * 2,
        out_specs=[WHOLE] * 2,
        scratch_shapes=[
            VMEM((latitudes, 2 * KW, lanes), f32),
            VMEM((half_groups, latitudes * KW, 2 * GROUP_LANES), f32),
            VMEM((2, 2, half_groups) + filters.shape[3:], f32),
            VMEM((2, half_groups, 2 * GROUP_LANES, 2 * GROUP_LANES), bf16),
            VMEM(state.shape, bf16),
            pltpu.SemaphoreType.DMA,
            pltpu.SemaphoreType.DMA,
        ],
        cost_estimate=cost(11),
        compiler_params=params(24),
    )(
        scalars,
        moved,
        far_state,
        norms,
        taken_norms,
        tables,
        near_grid,
        filters,
        taken_filters,
    )
    filtered, down_first, up_relayed, down_again = lax.optimization_barrier(
        (filtered, down_first, up_relayed, down)
    )
    down_second = send(down_again, far_diagonal)
    filtered_other = send(filtered, swap_cores)

    parts = 2
    partial, hidden = pl.pallas_call(
        functools.partial(hidden_kernel, rows // parts),
        out_shape=[
            VMEM((2 * rows, width, channels), f32),
            VMEM((2 * rows * ROW_STEP, hidden_half // 2), bf16),
        ],
        in_specs=[SCALARS] + [WHOLE] * 6 + [LEFT] * 7,
        out_specs=[WHOLE] * 2,
        scratch_shapes=[
            VMEM((2 * rows * ROW_STEP, channels), bf16),
            VMEM((channels, hidden_half), bf16),
            VMEM((hidden_half // 2, channels), bf16),
            pltpu.SemaphoreType.DMA((4,)),
            pltpu.SemaphoreType.DMA,
        ],
        cost_estimate=cost(11),
        compiler_params=params(26),
    )(
        scalars,
        near_base,
        far_base,
        filtered,
        filtered_other,
        norms,
        taken_norms,
        up_held,
        up_first,
        up_second,
        up_third,
        up_relayed,
        down,
        down_first,
    )
    landed, ready = [], []
    for number in range(parts):
        own, other = pl.pallas_call(
            functools.partial(update_kernel, number),
            out_shape=[
                jax.ShapeDtypeStruct((rows // parts, width, channels), f32),
                jax.ShapeDtypeStruct((rows // parts, width, channels), bf16),
            ],
            in_specs=[SCALARS] + [WHOLE] * 2 + [LEFT] * 2,
            out_specs=[WHOLE] * 2,
            scratch_shapes=[
                VMEM((hidden_half // 2, channels), bf16),
                pltpu.SemaphoreType.DMA,
            ],
            cost_estimate=cost(50),
            compiler_params=params(12),
        )(scalars, partial, hidden, down_first, down_second)
        ready.append((own + send(other, swap_cores).astype(f32)).astype(bf16))
        if number + 1 < parts:
            landed.append([send(ready[-1], onward_by_space)])
        else:
            landed.append([send(ready[-1], onward)])
    for number in range(parts - 1):
        first_hop = landed[number][0]
        if number > 0:
            first_hop, _ = lax.optimization_barrier((first_hop, ready[-1]))
        landed[number].append(send(first_hop, onward_rest))
    relayed = (core + space == 0).astype(i32)[None]
    out = pl.pallas_call(
        functools.partial(place_kernel, rows // parts * (parts - 1)),
        out_shape=jax.ShapeDtypeStruct(state.shape, bf16),
        in_specs=[WHOLE],
        out_specs=LEFT,
        scratch_shapes=[pltpu.SemaphoreType.DMA],
        cost_estimate=cost(100),
        compiler_params=params(16),
    )(landed[-1][0])
    arrived = [value for chunk in landed[:-1] for value in chunk]
    out = pl.pallas_call(
        collect_kernel,
        out_shape=jax.ShapeDtypeStruct(state.shape, bf16),
        in_specs=[SCALARS] + [WHOLE] * len(arrived) + [LEFT],
        out_specs=LEFT,
        input_output_aliases={1 + len(arrived): 0},
        scratch_shapes=[pltpu.SemaphoreType.DMA((parts - 1,))],
        compiler_params=params(16),
    )(relayed, *arrived, out)
    return out[None, None, None]


def solution(mesh):
    placed = (
        P("ens", "segment", None, "space", None, None),
        P("ens", None, None),
        P(),
        P("space", None, None),
        P(),
        P(),
        P("segment", None, None),
        P("segment", None, None),
        P("segment", None, None, None, None, None),
        P("segment", ("space", "ens"), None),
        P("segment", ("space", "ens"), None),
    )
    sizes = tuple(mesh.shape[axis] for axis in MESH_AXES)
    whole_micro_batch_on_a_chip = sizes[0] % 2 == 0 and sizes[1:] == (2, 2)
    if whole_micro_batch_on_a_chip:
        program = functools.partial(fast_on_device, sizes)
    else:
        program = on_device
    return jax.shard_map(
        program,
        mesh=mesh,
        in_specs=placed,
        out_specs=P("ens", "segment", None, "space", None, None),
        check_vma=False,
    )
```

```python
import functools
import math

import jax
import jax.numpy as jnp
import ml_dtypes
import numpy as np
from jax import lax
from jax.experimental import pallas as pl
from jax.experimental.pallas import tpu as pltpu
from jax.sharding import PartitionSpec as P

KW = 88


EPSILON = 1e-05
SHRINK_LEVEL = 0.01
HIGHEST_PRECISION = lax.Precision.HIGHEST


def shifted(value, axis, steps):
    count = lax.axis_size(axis)
    pairs = [(source, (source + steps) % count) for source in range(count)]
    return lax.ppermute(value, axis, pairs)


def layer_norm(values):
    average = jnp.mean(values, axis=-1, keepdims=True)
    centred = values - average
    spread = jnp.mean(centred * centred, axis=-1, keepdims=True)
    return centred * lax.rsqrt(spread + EPSILON)


def longitude_tables(longitudes, kept, latitudes):
    number = jnp.arange(kept, dtype=jnp.int32)[:, None]
    points = jnp.arange(longitudes, dtype=jnp.int32)[None, :]
    angles = (number * points % longitudes).astype(jnp.float32) * (2.0 * math.pi / longitudes)
    factor = 1.0 / math.sqrt(latitudes * longitudes)
    doubled = jnp.where(number == 0, 1.0, 2.0).astype(jnp.float32) * factor
    forward = jnp.stack([jnp.cos(angles) * factor, -jnp.sin(angles) * factor])
    backward = jnp.stack([jnp.cos(angles) * doubled, -jnp.sin(angles) * doubled])
    return (forward, backward)


def latitude_tables(latitudes):
    number = jnp.arange(latitudes, dtype=jnp.int32)[:, None]
    points = jnp.arange(latitudes, dtype=jnp.int32)[None, :]
    angles = (number * points % latitudes).astype(jnp.float32) * (2.0 * math.pi / latitudes)
    cosine_table = jnp.cos(angles)
    sine_table = jnp.sin(angles)
    forward = jnp.concatenate(
        [
            jnp.concatenate([cosine_table, sine_table], 1),
            jnp.concatenate([-sine_table, cosine_table], 1),
        ],
        0,
    )
    backward = jnp.concatenate(
        [
            jnp.concatenate([cosine_table, -sine_table], 1),
            jnp.concatenate([sine_table, cosine_table], 1),
        ],
        0,
    )
    return (forward, backward)


def mix_blocks(spectra, filters):
    extent = spectra.shape
    halves = spectra.reshape(extent[0], 2, extent[2], extent[3], filters.shape[2], filters.shape[3])
    nonimaginary_component = halves[:, 0]
    imag_part = halves[:, 1]

    def product(operand, matrix):
        return jnp.einsum("mhknb,nbc->mhknc", operand, matrix, precision=HIGHEST_PRECISION)

    first_real = jax.nn.relu(
        product(nonimaginary_component, filters[0, 0]) - product(imag_part, filters[0, 1])
    )
    first_imag = jax.nn.relu(
        product(nonimaginary_component, filters[0, 1]) + product(imag_part, filters[0, 0])
    )
    second_real = product(first_real, filters[1, 0]) - product(first_imag, filters[1, 1])
    second_imag = product(first_real, filters[1, 1]) + product(first_imag, filters[1, 0])
    blended = jnp.stack([second_real, second_imag], axis=1)
    blended = blended - jnp.clip(blended, -SHRINK_LEVEL, SHRINK_LEVEL)
    return blended.reshape(extent)


def spectral_filter(normed_one, filters, tables):
    forward, backward, lat_forward, lat_backward = tables
    spectra = jnp.einsum("rkw,mhwd->mrhkd", forward, normed_one, precision=HIGHEST_PRECISION)
    collected_fields = lax.all_to_all(spectra, "space", split_axis=3, concat_axis=2, tiled=True)
    extent = collected_fields.shape
    stacked = collected_fields.reshape(extent[0], 2 * extent[2], extent[3], extent[4])
    turned = jnp.einsum("ab,mbkd->makd", lat_forward, stacked, precision=HIGHEST_PRECISION)
    blended_modes = mix_blocks(turned.reshape(extent), filters).reshape(stacked.shape)
    inverse = jnp.einsum(
        "ab,mbkd->makd", lat_backward, blended_modes, precision=HIGHEST_PRECISION
    ).reshape(extent)
    returned = lax.all_to_all(inverse, "space", split_axis=2, concat_axis=3, tiled=True)
    return jnp.einsum("rkw,mrhkd->mhwd", backward, returned, precision=HIGHEST_PRECISION)


def on_device(
    state_in,
    member_ids,
    member_table,
    pos_embed,
    readout_tile_matrix,
    tile_lifting_matrix,
    norm_gain,
    norm_shift,
    spectral,
    up_weight,
    down_weight,
):
    position = lax.axis_index("segment")
    segment_count = lax.axis_size("segment")
    current = state_in[0, 0]
    channels = current.shape[3]
    latitudes = current.shape[1] * lax.axis_size("space")
    forward, backward = longitude_tables(current.shape[2], KW, latitudes)
    lat_forward, lat_backward = latitude_tables(latitudes)
    tables = (forward, backward, lat_forward, lat_backward)
    gains = norm_gain[0]
    shifts = norm_shift[0]
    filters = spectral[0]
    slot_index = -0 % segment_count
    chosen = member_ids[0, slot_index]
    onehot = (
        chosen[:, None] == jnp.arange(member_table.shape[0], dtype=jnp.int32)[None, :]
    ).astype(jnp.bfloat16)
    sample_trajectory_lines = jnp.dot(onehot, member_table, preferred_element_type=jnp.float32)

    def enter_grid(values):
        standardized_field = layer_norm(values.astype(jnp.float32)).astype(jnp.bfloat16)
        prediction_increment = jnp.einsum(
            "fbrd,do->fbro",
            standardized_field,
            readout_tile_matrix,
            preferred_element_type=jnp.float32,
        ).astype(jnp.bfloat16)
        admitted_lines = jnp.einsum(
            "nzwt,tl->nzwl",
            prediction_increment,
            tile_lifting_matrix,
            preferred_element_type=jnp.float32,
        )
        return (
            admitted_lines
            + pos_embed.astype(jnp.float32)[None]
            + sample_trajectory_lines[:, None, None, :]
        )

    def cast_values(values):
        return values.astype(jnp.float32)

    carried = lax.cond(position == 0, enter_grid, cast_values, current)
    normed_one = layer_norm(carried) * gains[0] + shifts[0]
    blended = carried + normed_one + spectral_filter(normed_one, filters, tables)
    normed_two = (layer_norm(blended) * gains[1] + shifts[1]).astype(jnp.bfloat16)
    flat_rows = normed_two.reshape(-1, channels)
    columns = flat_rows
    lifted = jnp.dot(
        columns,
        lax.all_gather(up_weight, ("space", "ens"), axis=1, tiled=True)[0],
        preferred_element_type=jnp.float32,
    )
    hidden = jax.nn.gelu(lifted, approximate=False).astype(jnp.bfloat16)
    columns = hidden
    update = jnp.dot(
        columns,
        lax.all_gather(down_weight, ("space", "ens"), axis=1, tiled=True)[0],
        preferred_element_type=jnp.float32,
    ).reshape(blended.shape)
    current = shifted((blended + update).astype(jnp.bfloat16), "segment", 1)
    return current[None, None]


ROW_STEP = 192
GROUP_LANES = 128
MESH_AXES = ("segment", "space", "ens")


def split_table(table):
    high = table.astype(ml_dtypes.bfloat16)
    low = (table - high.astype(np.float64)).astype(ml_dtypes.bfloat16)
    return np.stack([high, low])


def split_longitude_tables(longitudes, kept, latitudes):
    number = np.arange(kept)[:, None]
    points = np.arange(longitudes)[None, :]
    angles = (number * points % longitudes) * (2.0 * math.pi / longitudes)
    factor = 1.0 / math.sqrt(latitudes * longitudes)
    doubled = np.where(number == 0, 1.0, 2.0) * factor
    forward = np.concatenate([np.cos(angles) * factor, -np.sin(angles) * factor], 0)
    backward = np.concatenate([np.cos(angles) * doubled, -np.sin(angles) * doubled], 0).T
    size = max(forward.shape)
    both = np.zeros((2, size, size))
    both[0, : forward.shape[0], : forward.shape[1]] = forward
    both[1, : backward.shape[0], : backward.shape[1]] = backward
    return split_table(both)


def three_point(x, sign):
    (ar, ai), (br, bi), (cr, ci) = x
    tr, ti = br + cr, bi + ci
    mr, mi = ar - 0.5 * tr, ai - 0.5 * ti
    scale = math.sin(math.pi / 3.0) * sign
    dr, di = (br - cr) * scale, (bi - ci) * scale
    return [(ar + tr, ai + ti), (mr - di, mi + dr), (mr + di, mi - dr)]


def four_point(x, sign):
    (ar, ai), (br, bi), (cr, ci), (dr, di) = x
    sr, si, tr, ti = ar + cr, ai + ci, ar - cr, ai - ci
    ur, ui, vr, vi = br + dr, bi + di, br - dr, bi - di
    plus, minus = (tr - vi, ti + vr), (tr + vi, ti - vr)
    if sign < 0:
        plus, minus = minus, plus
    return [(sr + ur, si + ui), plus, (sr - ur, si - ui), minus]


def twelve_point(x, sign):
    columns = [three_point([x[(4 * a + 3 * b) % 12] for a in range(3)], sign) for b in range(4)]
    out = [None] * 12
    for a in range(3):
        line = four_point([columns[b][a] for b in range(4)], sign)
        for b in range(4):
            out[(4 * a + 9 * b) % 12] = line[b]
    return out


def lane_index(shape):
    return lax.broadcasted_iota(jnp.int32, shape, len(shape) - 1)


def spread_groups(values):
    a, b, c = (values[:, 128 * i : 128 * i + 128] for i in range(3))
    lanes = lane_index(a.shape)
    second = jnp.where(lanes < 32, pltpu.roll(a, 32, 1), pltpu.roll(b, 32, 1))
    third = jnp.where(lanes < 64, pltpu.roll(b, 64, 1), pltpu.roll(c, 64, 1))
    return jnp.concatenate([a, second, third, pltpu.roll(c, 96, 1)], 1)


def gather_groups(values):
    a, b, c, d = (values[:, 128 * i : 128 * i + 128] for i in range(4))
    lanes = lane_index(a.shape)
    first = jnp.where(lanes < 96, a, pltpu.roll(b, 96, 1))
    second = jnp.where(lanes < 64, pltpu.roll(b, 96, 1), pltpu.roll(c, 64, 1))
    third = jnp.where(lanes < 32, pltpu.roll(c, 64, 1), pltpu.roll(d, 32, 1))
    return jnp.concatenate([first, second, third], 1)


def gelu(x):
    return 0.5 * x * (1.0 + lax.erf(x * math.sqrt(0.5)))


def enter_kernel(
    scalars_ref,
    state_ref,
    readout_hbm,
    lifting_hbm,
    pos_hbm,
    table_hbm,
    out_ref,
    readout_ref,
    lifting_ref,
    pos_ref,
    table_ref,
    rows_ref,
    sems,
):
    first_segment, member = scalars_ref[0] == 0, scalars_ref[1]
    rows, width = state_ref.shape[:2]

    @pl.when(first_segment)
    def _():
        pairs = (
            (readout_hbm, readout_ref),
            (lifting_hbm, lifting_ref),
            (pos_hbm, pos_ref),
            (table_hbm, table_ref),
        )
        loads = [
            pltpu.make_async_copy(source, target, sems.at[number])
            for number, (source, target) in enumerate(pairs)
        ]
        for load in loads:
            load.start()
        rows_ref[...] = jnp.zeros_like(rows_ref)
        for row in range(rows):
            normed = layer_norm(state_ref[row].astype(jnp.float32)).astype(jnp.bfloat16)
            rows_ref[pl.ds(ROW_STEP * row, width)] = normed
        loads[0].wait()
        loads[3].wait()
        members = table_ref.shape[0]
        chosen = lax.broadcasted_iota(jnp.int32, (8, members), 1) == member
        line = jnp.dot(
            jnp.where(chosen, 1.0, 0.0).astype(jnp.bfloat16),
            table_ref[...],
            preferred_element_type=jnp.float32,
        )[0:1]
        for first in range(0, rows, 2):
            block = rows_ref[pl.ds(ROW_STEP * first, 2 * ROW_STEP)]
            forecast = jnp.dot(block, readout_ref[...], preferred_element_type=jnp.float32)
            if first == 0:
                loads[1].wait()
                loads[2].wait()
            lifted = jnp.dot(
                forecast.astype(jnp.bfloat16), lifting_ref[...], preferred_element_type=jnp.float32
            )
            for row in range(2):
                part = lifted[ROW_STEP * row : ROW_STEP * row + width]
                carried = part + pos_ref[first + row].astype(jnp.float32) + line
                out_ref[first + row] = carried.astype(jnp.bfloat16)

    @pl.when(jnp.logical_not(first_segment))
    def _():
        out_ref[...] = state_ref[...]


def load_one(near, near_ref, far_ref, target, sem):
    near_copy = pltpu.make_async_copy(near_ref, target, sem)
    far_copy = pltpu.make_async_copy(far_ref, target, sem)
    pl.when(near)(near_copy.start)
    pl.when(jnp.logical_not(near))(far_copy.start)
    return near_copy


def centre(values):
    average = jnp.mean(values, axis=-1, keepdims=True)
    centred = values - average
    spread = jnp.mean(centred * centred, axis=-1, keepdims=True)
    return centred, lax.rsqrt(spread + EPSILON)


def dot(a, b):
    return jnp.dot(a, b, preferred_element_type=jnp.float32)


def row_spectra(lower, centred, factor, norms, forward):
    channels = centred.shape[1] // 2

    def chosen(values):
        return jnp.where(lower, values[:, :channels], values[:, channels:])

    normed = chosen(centred) * factor * chosen(norms[0:1]) + chosen(norms[2:3])
    points = spread_groups(normed).astype(jnp.bfloat16)
    return dot(forward[0], points) + dot(forward[1], points)


def near_kernel(
    scalars_ref,
    entered_ref,
    near_state_ref,
    norms_ref,
    taken_norms_ref,
    tables_ref,
    grid_ref,
    base_ref,
    state_ref,
    sem,
):
    half, space = scalars_ref[0], scalars_ref[1]
    near = half == space
    load = load_one(near, entered_ref, near_state_ref, state_ref, sem)
    rows, width, _ = state_ref.shape
    norms = jnp.where(near, norms_ref[...], taken_norms_ref[...])
    forward = [tables_ref[part, 0, : grid_ref.shape[1], :width] for part in range(2)]
    load.wait()
    for row in range(rows):
        carried = state_ref[row].astype(jnp.float32)
        centred, factor = centre(carried)
        base_ref[row] = carried + (centred * factor * norms[0:1] + norms[2:3])
        grid_ref[row] = row_spectra(half == 0, centred, factor, norms, forward)


def filter_kernel(
    scalars_ref,
    moved_ref,
    far_state_ref,
    norms_ref,
    taken_norms_ref,
    tables_ref,
    near_grid_ref,
    filters_hbm,
    taken_filters_hbm,
    out_ref,
    base_ref,
    grid_ref,
    modes_ref,
    filters_ref,
    mixing_ref,
    state_ref,
    sem,
    state_sem,
):
    half, space = scalars_ref[0], scalars_ref[1]
    near = half == space
    rows, width, _ = state_ref.shape
    row_loads = start_loads(
        near,
        [far_state_ref.at[row] for row in range(rows)],
        [moved_ref.at[row] for row in range(rows)],
        [state_ref.at[row] for row in range(rows)],
        state_sem,
    )
    kept = grid_ref.shape[1] // 2
    groups = modes_ref.shape[0]
    side = filters_ref.shape[-1]
    wanted = pl.ds(half * groups, groups)
    own_load = load_one(
        near, filters_hbm.at[:, :, wanted], taken_filters_hbm.at[:, :, wanted], filters_ref, sem
    )
    norms = jnp.where(near, norms_ref[...], taken_norms_ref[...])
    odd_sign = jnp.where(space == 0, 1.0, -1.0)
    forward = [tables_ref[part, 0, : 2 * kept, :width] for part in range(2)]
    backward = [tables_ref[part, 1, :width, : 2 * kept] for part in range(2)]
    mixing_ref[...] = jnp.zeros_like(mixing_ref)
    for row in range(rows):
        row_loads[row].wait()
        carried = state_ref[row].astype(jnp.float32)
        centred, factor = centre(carried)
        base_ref[row] = carried + (centred * factor * norms[0:1] + norms[2:3])
        grid_ref[rows + row] = row_spectra(half == 0, centred, factor, norms, forward)
    own_load.wait()
    first, second = pl.ds(0, side), pl.ds(GROUP_LANES, side)
    for layer in range(2):
        for group in range(groups):
            real = filters_ref[layer, 0, group].astype(jnp.bfloat16)
            imag = filters_ref[layer, 1, group].astype(jnp.bfloat16)
            mixing_ref[layer, group, first, first] = real
            mixing_ref[layer, group, first, second] = imag
            mixing_ref[layer, group, second, first] = -imag
            mixing_ref[layer, group, second, second] = real

    def turn(step, carry):
        low = pl.multiple_of(step * 8, 8)
        for group in range(groups):
            lanes = pl.ds(GROUP_LANES * group, GROUP_LANES)
            values = []
            for h in range(12):
                source = near_grid_ref if h < rows else grid_ref
                values.append(
                    (source[h, pl.ds(low, 8), lanes], source[h, pl.ds(kept + low, 8), lanes])
                )
            for k, (real, imag) in enumerate(twelve_point(values, -1)):
                at = pl.ds(k * kept + low, 8)
                if k % 2 == 1:
                    real, imag = real * odd_sign, imag * odd_sign
                modes_ref[group, at, pl.ds(0, GROUP_LANES)] = real
                modes_ref[group, at, pl.ds(GROUP_LANES, GROUP_LANES)] = imag
        return carry

    lax.fori_loop(0, kept // 8, turn, 0)
    for group in range(groups):
        u = jax.nn.relu(dot(modes_ref[group].astype(jnp.bfloat16), mixing_ref[0, group]))
        v = dot(u.astype(jnp.bfloat16), mixing_ref[1, group])
        modes_ref[group] = v - jnp.clip(v, -SHRINK_LEVEL, SHRINK_LEVEL)

    def turn_back(step, carry):
        low = pl.multiple_of(step * 8, 8)
        for group in range(groups):
            lanes = pl.ds(GROUP_LANES * group, GROUP_LANES)
            values = []
            for k in range(12):
                at = pl.ds(k * kept + low, 8)
                real = modes_ref[group, at, pl.ds(0, GROUP_LANES)]
                imag = modes_ref[group, at, pl.ds(GROUP_LANES, GROUP_LANES)]
                if k % 2 == 1:
                    real, imag = real * odd_sign, imag * odd_sign
                values.append((real, imag))
            for h, (real, imag) in enumerate(twelve_point(values, 1)):
                grid_ref[h, pl.ds(low, 8), lanes] = real
                grid_ref[h, pl.ds(kept + low, 8), lanes] = imag
        return carry

    lax.fori_loop(0, kept // 8, turn_back, 0)
    for row in range(2 * rows):
        spectra = grid_ref[row].astype(jnp.bfloat16)
        filtered = dot(backward[0], spectra) + dot(backward[1], spectra)
        out_ref[row] = gather_groups(filtered).astype(out_ref.dtype)


def start_loads(near, near_refs, far_refs, targets, sems):
    def copies(refs):
        return [
            pltpu.make_async_copy(ref, target, sems.at[number])
            for number, (ref, target) in enumerate(zip(refs, targets))
        ]

    @pl.when(near)
    def _():
        for copy in copies(near_refs):
            copy.start()

    @pl.when(jnp.logical_not(near))
    def _():
        for copy in copies(far_refs):
            copy.start()

    return copies(near_refs)


def hidden_kernel(
    count,
    scalars_ref,
    near_base_ref,
    far_base_ref,
    mine_ref,
    theirs_ref,
    norms_ref,
    taken_norms_ref,
    held_ref,
    first_ref,
    second_ref,
    third_ref,
    relayed_ref,
    down_held_ref,
    down_first_ref,
    partial_ref,
    hidden_ref,
    rows_ref,
    up_ref,
    down_ref,
    sems,
    down_sem,
):
    half, space, member = scalars_ref[0], scalars_ref[1], scalars_ref[2]
    near = half == space
    rows, width, channels = near_base_ref.shape
    down_load = load_one(near, down_held_ref, down_first_ref, down_ref, down_sem)
    depth = held_ref.shape[0]
    here, away = 2 * space, 2 * (1 - space)
    order = [here + member, here + 1 - member, away + member, away + 1 - member]
    loads = start_loads(
        near,
        [held_ref, first_ref, second_ref, relayed_ref],
        [second_ref, third_ref, first_ref, relayed_ref],
        [up_ref.at[pl.ds(pl.multiple_of(shard * depth, depth), depth)] for shard in order],
        sems,
    )
    rows_ref[...] = jnp.zeros_like(rows_ref)
    norms = jnp.where(near, norms_ref[...], taken_norms_ref[...])

    def enter_row(part, row):
        mine = mine_ref[part * rows + row].astype(jnp.float32)
        theirs = theirs_ref[part * rows + row].astype(jnp.float32)
        low = jnp.where(half == 0, mine, theirs)
        high = jnp.where(half == 0, theirs, mine)
        base = (near_base_ref, far_base_ref)[part][row]
        blended = base + jnp.concatenate([low, high], 1)
        centred, factor = centre(blended)
        again = centred * factor * norms[1:2] + norms[3:4]
        place = row // count * 2 * count + part * count + row % count
        rows_ref[pl.ds(ROW_STEP * place, width)] = again.astype(jnp.bfloat16)
        own = near if part == 0 else jnp.logical_not(near)
        partial_ref[part * rows + row] = jnp.where(own, blended, 0.0)

    step = up_ref.shape[1] // 2
    columns = [pl.ds(pl.multiple_of(m * step, step), step) for m in (member, 1 - member)]
    for block in range(rows // count):
        for row in range(count * block, count * block + count):
            enter_row(0, row)
            enter_row(1, row)
        if block == 0:
            for copy in loads:
                copy.wait()
            down_load.wait()
        at = pl.ds(2 * count * ROW_STEP * block, 2 * count * ROW_STEP)
        values = rows_ref[at]
        hidden = gelu(dot(values, up_ref[:, columns[0]])).astype(jnp.bfloat16)
        update = dot(hidden, down_ref[...])
        for part in range(2):
            for row in range(count):
                start = ROW_STEP * (part * count + row)
                partial_ref[part * rows + count * block + row] += update[start : start + width]
        hidden_ref[at] = gelu(dot(values, up_ref[:, columns[1]])).astype(jnp.bfloat16)


def update_kernel(
    number,
    scalars_ref,
    partial_ref,
    hidden_ref,
    *rest,
):
    near = scalars_ref[0] == scalars_ref[1]
    if number == 0:
        first_ref, second_ref, own_ref, other_ref, down_ref, sem = rest
        load = load_one(near, first_ref, second_ref, down_ref, sem)
    else:
        down_ref, own_ref, other_ref = rest
    count, width, _ = own_ref.shape
    rows = partial_ref.shape[0] // 2
    size = count * ROW_STEP
    own_part = jnp.where(near, 0, 1)
    if number == 0:
        load.wait()
    for target, part in ((other_ref, 1 - own_part), (own_ref, own_part)):
        here = pl.ds(pl.multiple_of(2 * size * number + part * size, size), size)
        update = dot(hidden_ref[here], down_ref[...])
        for row in range(count):
            more = update[ROW_STEP * row : ROW_STEP * row + width]
            value = partial_ref[part * rows + count * number + row] + more
            target[row] = value.astype(target.dtype)


def place_kernel(start, chunk_ref, out_ref, sem):
    copy = pltpu.make_async_copy(chunk_ref, out_ref.at[pl.ds(start, chunk_ref.shape[0])], sem)
    copy.start()
    copy.wait()


def collect_kernel(relayed_ref, *refs):
    sources, out_ref, sems = refs[:-3], refs[-2], refs[-1]
    parts = len(sources) // 2
    count = sources[0].shape[0]

    def copies(step):
        return [
            pltpu.make_async_copy(
                sources[2 * part + step],
                out_ref.at[pl.ds(count * part, count)],
                sems.at[part],
            )
            for part in range(parts)
        ]

    for step in range(2):

        @pl.when(relayed_ref[0] == step)
        def _():
            for copy in copies(step):
                copy.start()

    for copy in copies(0):
        copy.wait()


VMEM = pltpu.VMEM
SCALARS = pl.BlockSpec(memory_space=pltpu.SMEM)
WHOLE = pl.BlockSpec(memory_space=pltpu.VMEM)
LEFT = pl.BlockSpec(memory_space=pltpu.HBM)


def cost(microseconds):
    return pl.CostEstimate(
        flops=int(microseconds * 2e8), bytes_accessed=0, transcendentals=0
    )


def params(megabytes):
    return pltpu.CompilerParams(vmem_limit_bytes=megabytes * 2**20)


def fast_on_device(
    sizes,
    state_in,
    member_ids,
    member_table,
    pos_embed,
    readout_tile_matrix,
    tile_lifting_matrix,
    norm_gain,
    norm_shift,
    spectral,
    up_weight,
    down_weight,
):
    segments, spaces, members = sizes
    position = lax.axis_index("segment")
    core = position % 2
    space = lax.axis_index("space")
    member = lax.axis_index("ens")
    near = core == space

    def table(target):
        pairs = []
        for g in range(segments):
            for s in range(spaces):
                for e in range(members):
                    to = target(g, s, e)
                    if to is not None:
                        flat = (to[0] * spaces + to[1]) * members + to[2]
                        pairs.append(((g * spaces + s) * members + e, flat))
        return pairs

    def send(value, pairs):
        return lax.ppermute(value, MESH_AXES, pairs)

    def keeps(g, s):
        return g % 2 == s

    def moved_place(g, s, e):
        return (g // 2 * 2 + s, g % 2, e)

    far_relocate = table(lambda g, s, e: None if keeps(g, s) else moved_place(g, s, e))
    first_way = table(lambda g, s, e: (g, s, 1 - e) if keeps(g, s) else moved_place(g, s, e))
    second_way = table(lambda g, s, e: (g ^ 1, s, e) if keeps(g, s) else (g, 1 - s, e))
    far_diagonal = table(
        lambda g, s, e: None if keeps(g, s) else moved_place(g, s, 1 - e)
    )
    across = table(lambda g, s, e: (g, s, 1 - e))
    third_way = table(lambda g, s, e: (g ^ 1, s, 1 - e) if keeps(g, s) else None)
    swap_cores = table(lambda g, s, e: (g ^ 1, s, e))
    onward = table(lambda g, s, e: ((g // 2 * 2 + s + 1) % segments, g % 2, e))
    onward_by_space = table(
        lambda g, s, e: (g, 0, e)
        if s == 1 and g % 2 == 0
        else ((g // 2 * 2 + s + 1) % segments, g % 2, e)
    )
    onward_rest = table(
        lambda g, s, e: ((g + 2) % segments, 0, e) if s == 0 and g % 2 == 0 else None
    )

    state = state_in[0, 0, 0]
    rows, width, channels = state.shape
    latitudes = rows * spaces
    bf16, f32, i32 = jnp.bfloat16, jnp.float32, jnp.int32
    up, down = up_weight[0], down_weight[0]
    hidden_half = up.shape[1] // 2

    up_held = lax.dynamic_slice_in_dim(up, space * hidden_half, hidden_half, 1)
    up_held, up_again = lax.optimization_barrier((up_held, up))
    up_given = lax.dynamic_slice_in_dim(up_again, (1 - space) * hidden_half, hidden_half, 1)
    up_first = send(up_held, first_way)
    up_second = send(up_given, second_way)
    entered = pl.pallas_call(
        enter_kernel,
        out_shape=VMEM(state.shape, bf16),
        in_specs=[SCALARS, WHOLE] + [LEFT] * 4,
        out_specs=WHOLE,
        scratch_shapes=[
            VMEM(readout_tile_matrix.shape, bf16),
            VMEM(tile_lifting_matrix.shape, bf16),
            VMEM(pos_embed.shape, bf16),
            VMEM(member_table.shape, bf16),
            VMEM((rows * ROW_STEP, channels), bf16),
            pltpu.SemaphoreType.DMA((4,)),
        ],
        cost_estimate=cost(9),
        compiler_params=params(58),
    )(
        jnp.stack([position, member_ids[0, 0, 0]]).astype(i32),
        state,
        readout_tile_matrix,
        tile_lifting_matrix,
        pos_embed,
        member_table,
    )
    up_third = send(up_given, third_way)
    entered, up_first, up_second, up_third = lax.optimization_barrier(
        (entered, up_first, up_second, up_third)
    )
    moved = send(entered, far_relocate)
    near_state = send(entered, swap_cores)
    up_relayed = send(jnp.where(near, up_second, up_first), across)
    norms = jnp.concatenate([norm_gain[0], norm_shift[0]], 0)
    taken_norms = send(norms, swap_cores)
    filters = spectral[0]
    taken_filters = send(filters, swap_cores)
    scalars = jnp.stack([core, space, member]).astype(i32)
    tables = jnp.asarray(split_longitude_tables(width, KW, latitudes))
    half_groups = spectral.shape[3] // 2
    lanes = half_groups * GROUP_LANES
    near_grid, near_base = pl.pallas_call(
        near_kernel,
        out_shape=[VMEM((rows, 2 * KW, lanes), f32), VMEM(state.shape, f32)],
        in_specs=[SCALARS] + [LEFT] * 2 + [WHOLE] * 3,
        out_specs=[WHOLE] * 2,
        scratch_shapes=[VMEM(state.shape, bf16), pltpu.SemaphoreType.DMA],
        cost_estimate=cost(5),
        compiler_params=params(12),
    )(scalars, entered, near_state, norms, taken_norms, tables)
    moved, near_grid, up_relayed, taken_filters, down_later = lax.optimization_barrier(
        (moved, near_grid, up_relayed, taken_filters, down)
    )
    far_state = send(moved, swap_cores)
    down_first = send(down_later, first_way)
    filtered, far_base = pl.pallas_call(
        filter_kernel,
        out_shape=[
            jax.ShapeDtypeStruct((2 * rows, width, channels // 2), bf16),
            VMEM(state.shape, f32),
        ],
        in_specs=[SCALARS] + [LEFT] * 2 + [WHOLE] * 4 + [LEFT] * 2,
        out_specs=[WHOLE] * 2,
        scratch_shapes=[
            VMEM((latitudes, 2 * KW, lanes), f32),
            VMEM((half_groups, latitudes * KW, 2 * GROUP_LANES), f32),
            VMEM((2, 2, half_groups) + filters.shape[3:], f32),
            VMEM((2, half_groups, 2 * GROUP_LANES, 2 * GROUP_LANES), bf16),
            VMEM(state.shape, bf16),
            pltpu.SemaphoreType.DMA,
            pltpu.SemaphoreType.DMA((rows,)),
        ],
        cost_estimate=cost(11),
        compiler_params=params(24),
    )(
        scalars,
        moved,
        far_state,
        norms,
        taken_norms,
        tables,
        near_grid,
        filters,
        taken_filters,
    )
    filtered, down_first, up_relayed, down_again = lax.optimization_barrier(
        (filtered, down_first, up_relayed, down)
    )
    down_second = send(down_again, far_diagonal)
    filtered_other = send(filtered, swap_cores)

    parts = 2
    partial, hidden = pl.pallas_call(
        functools.partial(hidden_kernel, rows // parts),
        out_shape=[
            VMEM((2 * rows, width, channels), f32),
            VMEM((2 * rows * ROW_STEP, hidden_half // 2), bf16),
        ],
        in_specs=[SCALARS] + [WHOLE] * 6 + [LEFT] * 7,
        out_specs=[WHOLE] * 2,
        scratch_shapes=[
            VMEM((2 * rows * ROW_STEP, channels), bf16),
            VMEM((channels, hidden_half), bf16),
            VMEM((hidden_half // 2, channels), bf16),
            pltpu.SemaphoreType.DMA((4,)),
            pltpu.SemaphoreType.DMA,
        ],
        cost_estimate=cost(11),
        compiler_params=params(26),
    )(
        scalars,
        near_base,
        far_base,
        filtered,
        filtered_other,
        norms,
        taken_norms,
        up_held,
        up_first,
        up_second,
        up_third,
        up_relayed,
        down,
        down_first,
    )
    landed, ready = [], []
    for number in range(parts):
        sums = [
            jax.ShapeDtypeStruct((rows // parts, width, channels), f32),
            jax.ShapeDtypeStruct((rows // parts, width, channels), bf16),
        ]
        if number == 0:
            shapes = sums + [VMEM((hidden_half // 2, channels), bf16)]
            weights, specs = (down_first, down_second), [LEFT] * 2
            scratch = [pltpu.SemaphoreType.DMA]
        else:
            shapes, weights, specs, scratch = sums, (down_last,), [WHOLE], []
        own, other, *handed = pl.pallas_call(
            functools.partial(update_kernel, number),
            out_shape=shapes,
            in_specs=[SCALARS] + [WHOLE] * 2 + specs,
            out_specs=[WHOLE] * len(shapes),
            scratch_shapes=scratch,
            cost_estimate=cost(50),
            compiler_params=params(12),
        )(scalars, partial, hidden, *weights)
        down_last = handed[0] if handed else down_last
        ready.append((own + send(other, swap_cores).astype(f32)).astype(bf16))
        if number + 1 < parts:
            landed.append([send(ready[-1], onward_by_space)])
        else:
            landed.append([send(ready[-1], onward)])
    for number in range(parts - 1):
        first_hop = landed[number][0]
        if number > 0:
            first_hop, _ = lax.optimization_barrier((first_hop, ready[-1]))
        landed[number].append(send(first_hop, onward_rest))
    relayed = (core + space == 0).astype(i32)[None]
    out = pl.pallas_call(
        functools.partial(place_kernel, rows // parts * (parts - 1)),
        out_shape=jax.ShapeDtypeStruct(state.shape, bf16),
        in_specs=[WHOLE],
        out_specs=LEFT,
        scratch_shapes=[pltpu.SemaphoreType.DMA],
        cost_estimate=cost(100),
        compiler_params=params(16),
    )(landed[-1][0])
    arrived = [value for chunk in landed[:-1] for value in chunk]
    out = pl.pallas_call(
        collect_kernel,
        out_shape=jax.ShapeDtypeStruct(state.shape, bf16),
        in_specs=[SCALARS] + [WHOLE] * len(arrived) + [LEFT],
        out_specs=LEFT,
        input_output_aliases={1 + len(arrived): 0},
        scratch_shapes=[pltpu.SemaphoreType.DMA((parts - 1,))],
        compiler_params=params(16),
    )(relayed, *arrived, out)
    return out[None, None, None]


def solution(mesh):
    placed = (
        P("ens", "segment", None, "space", None, None),
        P("ens", None, None),
        P(),
        P("space", None, None),
        P(),
        P(),
        P("segment", None, None),
        P("segment", None, None),
        P("segment", None, None, None, None, None),
        P("segment", ("space", "ens"), None),
        P("segment", ("space", "ens"), None),
    )
    sizes = tuple(mesh.shape[axis] for axis in MESH_AXES)
    whole_micro_batch_on_a_chip = sizes[0] % 2 == 0 and sizes[1:] == (2, 2)
    if whole_micro_batch_on_a_chip:
        program = functools.partial(fast_on_device, sizes)
    else:
        program = on_device
    return jax.shard_map(
        program,
        mesh=mesh,
        in_specs=placed,
        out_specs=P("ens", "segment", None, "space", None, None),
        check_vma=False,
    )
```
